128 devices in a mesh: sub: 32 (over z, x, core), col: 4 (over y).
Axes of the slice: x: 4, y: 4, z: 4, core: 2. Of those that a mesh axis runs over, the one named last changes fastest.
Arguments:
- elem_records: bfloat16 [32768, 1152], P(('sub', 'col')), may hold values from -0.119628906 to 0.119628906
- elem_owner: int32 [32768, 1], P(('sub', 'col')), may hold values from 0 to 31; in each aligned block of 256 rows (0 to 255, 256 to 511, ...) at most 16 rows name the same one
- elem_block: int32 [32768], P(('sub', 'col')), may hold values from 0 to 255
- elem_offset: int32 [32768], P(('sub', 'col')), may hold values from 0 to 5
- modes: bfloat16 [512, 64, 512], P('sub', None, 'col'), may hold values from -0.59765625 to 0.59765625
- mode_readers: int32 [512, 2], P('sub'), may hold values from 0 to 31, all different within a row; in each aligned block of 16 rows (0 to 15, 16 to 31, ...) at most 2 rows name the same one
- pattern: int32 [2048, 4], P('sub'), may hold values from 0 to 63
Outputs:
- gram_stiff: float32 [512, 512], P('sub', 'col')
- gram_mass: float32 [512, 512], P('sub', 'col')
The draws below stay inside these ranges and needn't reach their ends.
Inputs may be any that keep to these rules, and one draw needn't show every extreme that they name: `elem_owner`: the rows of one device name one subdomain at most 16 times, and in every draw some subdomain exactly 16 times. `mode_readers`: each row names two different subdomains; the rows of one index of sub name one subdomain at most 2 times, and in every draw some subdomain exactly 2 times.
All inputs are finite; a program needn't handle non-finite values.
Results may differ from the reference program's by a relative error of at most 0.0038.
Values may be sent and summed in bfloat16 or wider, within the bound.
A program may use at most 192 MiB of HBM per device.

```python
import math
import jax
import jax.numpy as jnp
import numpy as np
from jax import lax

MODES = 512
BS = 64
EDOF = 24
NNZ = 4
E_DEV = 256
QB_DEV = 16
NQ = 64
CAPQ = 2
CAPE = 16
KW = 1152
ELEMS = 32768
BLOCKS = 512
SLOTS = 2048
N_SUB = 32
N_COL = 4


def touch_ends(drawn, own_key, low, top_value):
    longest = drawn.shape.index(max(drawn.shape))
    spots = []
    for shift in (0, 1):
        where = [jax.random.randint(jax.random.fold_in(own_key, axis), (), 0, length) for axis, length in enumerate(drawn.shape)]
        where[longest] = (where[longest] + shift) % drawn.shape[longest]
        spots.append(tuple(where))
    return drawn.at[spots[0]].set(low).at[spots[1]].set(top_value)


def block_scale(rng, dims, split, low, high):
    level, own = 1.0, jax.random.fold_in(rng, 6)
    for axis_at, parts in split:
        steps = jnp.exp(jax.random.uniform(jax.random.fold_in(own, axis_at), (parts,), jnp.float32, low / len(split), high / len(split)))
        level = level * jnp.repeat(steps, dims[axis_at] // parts).reshape([-1 if axis == axis_at else 1 for axis in range(len(dims))])
    return level


def deal_out(key, own, number, rows, amount, top, most, slope):
    ranking = jax.random.permutation(key, amount)
    crowded, ordinary = shares(amount, rows * top, most, slope, True), shares(amount, rows * top, most, slope, False)
    places = jnp.arange(amount)

    def named(tallies, rotation):
        used = int((tallies > 0).sum())
        fixed = max(1, used // 4)
        moved = fixed + (places - fixed + rotation * (used - fixed)) % max(1, amount - fixed)
        return jnp.zeros((amount,), jnp.int32).at[ranking[jnp.where(places < fixed, places, moved)]].set(jnp.asarray(tallies, jnp.int32))

    tallies = jnp.where(number % 4 == 0, named(crowded, number // 4), named(ordinary, number - number // 4 - 1))
    mixed = jax.random.permutation(jax.random.fold_in(own, 3), amount)
    donor, sink = mixed[0:amount // 2 * 2:2], mixed[1:amount // 2 * 2:2]
    margin = jnp.minimum(tallies[donor] - 1, most - tallies[sink]) // 2
    margin = jnp.where((donor == ranking[0]) | (sink == ranking[0]) | (tallies[sink] == 0), 0, jnp.maximum(margin, 0))
    moved = jax.random.randint(jax.random.fold_in(own, 4), (amount // 2,), 0, 1 << 20) % (margin + 1)
    tallies = tallies.at[donor].add(-moved).at[sink].add(moved)
    labels = jnp.searchsorted(jnp.cumsum(tallies), jnp.arange(rows * top), side="right").astype(jnp.int32)
    grid = labels.reshape(top, rows).T
    grid = grid[jax.random.permutation(jax.random.fold_in(own, 1), rows)]
    rotation = jax.random.randint(jax.random.fold_in(own, 2), (rows, 1), 0, top)
    return jnp.take_along_axis(grid, (jnp.arange(top)[None, :] + rotation) % top, axis=1)


def shares(amount, total, reach, slope, full):
    weights = [(1 << 20) // math.isqrt(standing ** slope) + 1 for standing in range(1, amount + 1)]
    largest = reach if full else min(reach, max(-(-total // amount), total * weights[0] // sum(weights)))
    least = 1 if total - largest >= amount - 1 else 0
    given, rest = [largest] + [least] * (amount - 1), total - largest - least * (amount - 1)
    while rest > 0:
        candidates = [i for i in range(1, amount) if given[i] < largest] or [i for i in range(1, amount) if given[i] < reach]
        whole, left = sum([weights[i] for i in candidates]), rest
        for i in candidates:
            extra = min(reach - given[i], max(1, left * weights[i] // whole), rest)
            given[i] = given[i] + extra
            rest = rest - extra
    return np.array(given)


def centred(rng, extent, spread, limit, cuts=(), held_as=jnp.bfloat16):
    array = jax.random.normal(rng, extent, jnp.float32) * spread
    if len(cuts) > 0:
        array = block_scale(rng, extent, cuts, -0.22, 0.18) * array
    return jnp.clip(array, min=-limit, max=limit).astype(held_as)


def setup_inputs(seed: int = 0) -> dict:
    key_list = jax.random.split(jax.random.key(seed), 8)
    elem_records = centred(key_list[0], (ELEMS, KW), 0.02, 0.119628906, ((0, 128),))
    elem_owner_keys = jax.random.split(jax.random.fold_in(key_list[1], 1), ELEMS // E_DEV)
    elem_owner_turns = jax.random.permutation(jax.random.fold_in(key_list[1], 3), ELEMS // E_DEV)
    elem_owner = jax.vmap(lambda own, number: deal_out(jax.random.fold_in(key_list[1], 2), own, number, E_DEV, N_SUB, 1, CAPE, 2))(elem_owner_keys, elem_owner_turns).reshape((ELEMS, 1))
    elem_block = touch_ends(jax.random.randint(key_list[2], (ELEMS,), 0, NQ * NNZ), jax.random.fold_in(key_list[2], 1), 0, (NQ * NNZ) - 1).astype(jnp.int32)
    elem_offset = touch_ends(jax.random.randint(key_list[3], (ELEMS,), 0, 6), jax.random.fold_in(key_list[3], 1), 0, 5).astype(jnp.int32)
    modes = centred(key_list[4], (BLOCKS, BS, MODES), 0.1, 0.59765625, ((0, 32), (2, 4)))
    mode_readers_keys = jax.random.split(jax.random.fold_in(key_list[5], 1), BLOCKS // QB_DEV)
    mode_readers_turns = jax.random.permutation(jax.random.fold_in(key_list[5], 3), BLOCKS // QB_DEV)
    mode_readers = jax.vmap(lambda own, number: deal_out(jax.random.fold_in(key_list[5], 2), own, number, QB_DEV, N_SUB, 2, CAPQ, 1))(mode_readers_keys, mode_readers_turns).reshape((BLOCKS, 2))
    pattern = touch_ends(jax.random.randint(key_list[6], (SLOTS, NNZ), 0, NQ), jax.random.fold_in(key_list[6], 1), 0, NQ - 1).astype(jnp.int32)
    return {"elem_records": elem_records, "elem_owner": elem_owner, "elem_block": elem_block, "elem_offset": elem_offset, "modes": modes, "mode_readers": mode_readers, "pattern": pattern}


def place_index(block_ids, offsets, slot_count, entry_count):
    entries = jnp.arange(EDOF * EDOF, dtype=jnp.int32)
    row_part = entries // EDOF
    col_part = entries % EDOF
    shifted = offsets[:, None] * 8
    base_index = block_ids[:, None] * (BS * BS) + (shifted + row_part[None, :]) * BS + shifted + col_part[None, :]
    return jnp.concatenate([base_index, base_index + slot_count * entry_count * BS * BS], axis=1)


def reference(elem_records, elem_owner, elem_block, elem_offset, modes, mode_readers, pattern):
    owners = elem_owner[:, 0]
    order = jnp.argsort(owners, stable=True)
    most_per = 2 * E_DEV * N_COL
    sorted_records = jnp.concatenate([elem_records[order], jnp.zeros((most_per, KW), elem_records.dtype)], axis=0)
    sorted_block = jnp.concatenate([elem_block[order], jnp.zeros((most_per,), jnp.int32)], axis=0)
    sorted_offset = jnp.concatenate([elem_offset[order], jnp.zeros((most_per,), jnp.int32)], axis=0)
    readers_flat = mode_readers.reshape(-1)
    total_size = 2 * NQ * NNZ * BS * BS

    def per_sub(carry, sub_id):
        start_at = jnp.sum((owners < sub_id).astype(jnp.int32)).astype(jnp.int32)
        live_count = jnp.sum((owners == sub_id).astype(jnp.int32))
        records = lax.dynamic_slice_in_dim(sorted_records, start_at, most_per, 0)
        blocks_here = lax.dynamic_slice_in_dim(sorted_block, start_at, most_per, 0)
        offsets_here = lax.dynamic_slice_in_dim(sorted_offset, start_at, most_per, 0)
        valid = jnp.arange(most_per, dtype=jnp.int32) < live_count
        flat = place_index(blocks_here, offsets_here, NQ, NNZ)
        flat = jnp.where(valid[:, None], flat, total_size)
        assembled = jnp.zeros((total_size,), jnp.float32).at[flat.reshape(-1)].add(
            records.astype(jnp.float32).reshape(-1), mode="drop")
        stiff_mass = assembled.reshape(2, NQ, NNZ, BS, BS).astype(jnp.bfloat16)
        matches = (readers_flat == sub_id).reshape(N_SUB, QB_DEV * 2).astype(jnp.int32)
        ranks = jnp.cumsum(matches, axis=1) - 1
        targets = jnp.arange(N_SUB, dtype=jnp.int32)[:, None] * CAPQ + ranks
        slots = jnp.where(matches > 0, targets, NQ).reshape(-1).astype(jnp.int32)
        entry_ids = jnp.arange(BLOCKS * 2, dtype=jnp.int32)
        slot_entry = jnp.full((NQ,), -1, jnp.int32).at[slots].set(entry_ids, mode="drop")
        filled = slot_entry >= 0
        picked = modes[jnp.maximum(slot_entry, 0) // 2]
        slot_modes = jnp.where(filled[:, None, None], picked, jnp.zeros_like(picked))
        local_pattern = lax.dynamic_slice_in_dim(pattern, (sub_id * NQ).astype(jnp.int32), NQ, 0)
        gathered = slot_modes[local_pattern]
        products = jnp.einsum("crjab,rjbm->cram", stiff_mass.astype(jnp.float32),
                              gathered.astype(jnp.float32)).astype(jnp.bfloat16)
        mode_rows = slot_modes.reshape(NQ * BS, MODES)
        stiff_term = jnp.dot(mode_rows.T, products[0].reshape(NQ * BS, MODES), preferred_element_type=jnp.float32)
        mass_term = jnp.dot(mode_rows.T, products[1].reshape(NQ * BS, MODES), preferred_element_type=jnp.float32)
        return (carry[0] + stiff_term, carry[1] + mass_term), None

    start_sums = (jnp.zeros((MODES, MODES), jnp.float32), jnp.zeros((MODES, MODES), jnp.float32))
    sums, unused = lax.scan(per_sub, start_sums, jnp.arange(N_SUB, dtype=jnp.int32))
    return sums[0], sums[1]
```

```python
import functools

import jax
import jax.numpy as jnp
from jax import lax
from jax.experimental import pallas as pl
from jax.experimental.pallas import tpu as pltpu
from jax.sharding import PartitionSpec as P

MESH = pl.DeviceIdType.MESH
BF16 = jnp.bfloat16
F32 = jnp.float32
I32 = jnp.int32

BS = 64
NQ = 64
NNZ = 4
KW = 1152
KA = 1280
COLS = 128
SLOTS_E = 16


def dot(a, b):
    return jnp.dot(a, b, preferred_element_type=F32)


def dot_nt(a, b):
    return lax.dot_general(a, b, (((1,), (1,)), ((), ())), preferred_element_type=F32)


def kernel(
    midx, pat, rec, place, owner_row, owner_col, modes,
    stiff, mass,
    send_m, x0, xl, xr, xo, send_r, rbuf, ebuf, mbuf, ks, lb, xt, pb, gst, d0, hs, hr, tot, tr,
    sm_send, sm_recv, sr_send, sr_recv, fr_send, fl_send, xl_recv, xr_recv,
    rr_send, rl_send, xoa_recv, xob_recv, d_send, d_recv, h_send, h_recv, t_send, t_recv,
):
    me = lax.axis_index("sub")
    y = lax.axis_index("col")
    core = lax.rem(me, 2)
    p = me // 2
    z = p // 4
    x = lax.rem(p, 4)
    sib = p * 2 + 1 - core
    right = lax.rem(y + 1, 4)
    left = lax.rem(y + 3, 4)
    opp = lax.rem(y + 2, 4)

    def chip_at(g):
        return lax.rem(z + g // 4, 4) * 4 + lax.rem(x + lax.rem(g, 4), 4)

    def chip_from(g):
        return lax.rem(z + 4 - g // 4, 4) * 4 + lax.rem(x + 4 - lax.rem(g, 4), 4)

    def remote(src, dst, ssem, rsem, dev):
        return pltpu.make_async_remote_copy(
            src_ref=src, dst_ref=dst, send_sem=ssem, recv_sem=rsem, device_id=dev, device_id_type=MESH
        )

    def wait_bytes(ref, sem):
        pltpu.make_async_copy(ref, ref, sem).wait()

    barrier = pltpu.get_barrier_semaphore()
    pl.semaphore_signal(barrier, inc=1, device_id=(sib, y), device_id_type=MESH)
    for yy in (left, right, opp):
        pl.semaphore_signal(barrier, inc=1, device_id=(me, yy), device_id_type=MESH)

    def greet(g, _):
        q = chip_at(g)
        for cc in range(2):
            pl.semaphore_signal(barrier, inc=1, device_id=(q * 2 + cc, y), device_id_type=MESH)
        return 0

    lax.fori_loop(1, 16, greet, 0)

    def fill(s, _):
        k = midx[s]
        block = modes[jnp.maximum(k, 0)]
        send_m[s] = jnp.where(k >= 0, block, jnp.zeros_like(block))
        return 0

    lax.fori_loop(0, NQ, fill, 0, unroll=4)
    pl.semaphore_wait(barrier, 34)

    x0[pl.ds(2 * me, 2)] = send_m[pl.ds(2 * me, 2)]

    def send_mode(dest):
        remote(
            send_m.at[pl.ds(2 * dest, 2)], x0.at[pl.ds(2 * me, 2)], sm_send, sm_recv.at[p], (dest, y)
        ).start()

    send_mode(sib)

    def send_modes(g, _):
        q = chip_at(g)
        for cc in range(2):
            send_mode(q * 2 + cc)
        return 0

    lax.fori_loop(1, 16, send_modes, 0)

    before = lax.broadcasted_iota(I32, (256, 256), 0) < lax.broadcasted_iota(I32, (256, 256), 1)
    same = owner_col[...] == owner_row[...]
    rank = jnp.sum(jnp.where(same & before, 1, 0), axis=0, keepdims=True)
    pos = owner_row[...] * SLOTS_E + rank

    def permute(g, _):
        rows = lax.broadcasted_iota(I32, (128, 256), 0) + g * 128
        pick = jnp.where(rows == pos, 1.0, 0.0).astype(BF16)
        at = pl.ds(pl.multiple_of(g * 128, 128), 128)
        send_r[at, 0:KW] = dot(pick, rec[...]).astype(BF16)
        send_r[at, KW:KA] = dot(pick, place[...]).astype(BF16)
        return 0

    lax.fori_loop(0, 4, permute, 0)

    def rows16(d):
        return pl.ds(pl.multiple_of(d * 16, 16), 16)

    rbuf[rows16(me)] = send_r[rows16(me)]

    def send_rec(dest):
        remote(send_r.at[rows16(dest)], rbuf.at[rows16(me)], sr_send, sr_recv, (dest, y)).start()

    send_rec(sib)

    def send_recs(g, _):
        q = chip_at(g)
        for cc in range(2):
            send_rec(q * 2 + cc)
        return 0

    lax.fori_loop(1, 16, send_recs, 0)

    def forward(q):
        at = pl.ds(4 * q, 4)
        remote(x0.at[at], xl.at[at], fr_send, xl_recv.at[q], (me, right)).start()
        remote(x0.at[at], xr.at[at], fl_send, xr_recv.at[q], (me, left)).start()

    def relay(q):
        at = pl.ds(4 * q, 4)
        lo = pl.ds(4 * q, 2)
        hi = pl.ds(4 * q + 2, 2)
        wait_bytes(xl.at[at], xl_recv.at[q])
        remote(xl.at[lo], xo.at[lo], rr_send, xoa_recv, (me, right)).start()
        wait_bytes(xr.at[at], xr_recv.at[q])
        remote(xr.at[hi], xo.at[hi], rl_send, xob_recv, (me, left)).start()

    wait_bytes(x0.at[pl.ds(2 * sib, 2)], sm_recv.at[p])
    forward(p)

    def forwards(g, _):
        q = chip_from(g)
        wait_bytes(x0.at[pl.ds(4 * q, 4)], sm_recv.at[q])
        forward(q)
        return 0

    lax.fori_loop(1, 16, forwards, 0)

    def relays(g, _):
        relay(chip_from(g))
        return 0

    def place_matrix(n, _):
        ri = n // 6
        o = lax.rem(n, 6)
        k = lax.broadcasted_iota(I32, (256, 256), 0)
        col = lax.broadcasted_iota(I32, (256, 256), 1)
        bb = (col & 63) - 8 * o
        hit = (k == 32 * ri + (col >> 6) * 24 + bb) & (bb >= 0) & (bb < 24)
        ebuf[n] = jnp.where(hit, 1.0, 0.0).astype(BF16)
        return 0

    lax.fori_loop(0, 24, place_matrix, 0)
    for o in (0, 1, 8, 9):
        mbuf[o] = jnp.zeros((256, KA), BF16)

    lax.fori_loop(0, 8, relays, 0)

    wait_bytes(rbuf.at[pl.ds(0, 31 * 16)], sr_recv)
    lane = lax.broadcasted_iota(I32, (8, 128), 1)
    rowi = lax.broadcasted_iota(I32, (8, 128), 0)
    pickrow = jnp.where(lane == rowi, 1.0, 0.0).astype(BF16)
    where = dot_nt(pickrow, rbuf[:, KW:KA]).astype(I32)
    blk = where[0:1]
    key = where[1:2] * 256 + (blk & 3) * 64 + (blk >> 2)

    def collect(o, _):
        rows = lax.broadcasted_iota(I32, (256, 512), 0) + o * 256
        pick = jnp.where(rows == key, 1.0, 0.0).astype(BF16)
        mbuf[o + 2] = dot(pick, rbuf[...]).astype(BF16)
        return 0

    lax.fori_loop(0, 6, collect, 0)

    lax.fori_loop(8, 16, relays, 0)

    def assemble(v, _):
        for c in range(2):
            for w in range(2):
                acc = None
                for d in range(3):
                    first = c * 576 + 96 * (w + 2 * d)
                    base = first // 128 * 128
                    ri = (first - base) // 32
                    term = dot(
                        mbuf[v - d + 2, :, base : base + 256],
                        ebuf[ri * 6 + jnp.clip(v - d, 0, 5)],
                    )
                    acc = term if acc is None else acc + term
                for a4 in range(4):
                    row = c * 64 + 8 * v + 4 * w + a4
                    at = pl.ds(pl.multiple_of(row * 64, 64), 64)
                    for h in range(2):
                        ks[h, at, :] = jnp.concatenate(
                            [
                                acc[j * 64 : j * 64 + 64, a4 * 64 : a4 * 64 + 64]
                                for j in (2 * h, 2 * h + 1)
                            ],
                            axis=1,
                        )
        return 0

    lax.fori_loop(0, 8, assemble, 0)

    def gather_rows(i, _):
        for h in range(2):
            lb[i, :, h * 128 : h * 128 + 128] = ks[h, pl.ds(i, 128, stride=64), :].astype(BF16)
        return 0

    lax.fori_loop(0, 64, gather_rows, 0)

    eye = jnp.where(
        lax.broadcasted_iota(I32, (128, 128), 0) == lax.broadcasted_iota(I32, (128, 128), 1), 1.0, 0.0
    ).astype(BF16)

    def transpose(ref, q):
        def one(g, _):
            part = ref[pl.ds(4 * g, 4)].reshape(256, COLS)
            xt[q * 128 : q * 128 + 128, pl.ds(pl.multiple_of(g * 256, 256), 256)] = dot_nt(eye, part).astype(BF16)
            return 0

        lax.fori_loop(0, 16, one, 0)

    def multiply(parts):
        def one(i, _):
            ids = [pat[4 * i + j] for j in range(4)]
            right_side = jnp.concatenate(
                [jnp.concatenate([ref[n] for n in ids], axis=0) for ref, _ in parts], axis=1
            )
            out = dot(lb[i], right_side).astype(BF16)
            at = pl.ds(pl.multiple_of(i * 64, 64), 64)
            for n, (_, q) in enumerate(parts):
                pb[q, at, 0:128] = out[0:64, n * 128 : n * 128 + 128]
                pb[q, at, 128:256] = out[64:128, n * 128 : n * 128 + 128]
            return 0

        lax.fori_loop(0, 64, one, 0)

    transpose(x0, 0)
    transpose(xl, 1)
    transpose(xr, 2)
    multiply([(x0, 0), (xl, 1)])
    lo = xo.at[pl.ds(0, 32)]
    wait_bytes(lo, xoa_recv)
    wait_bytes(lo, xob_recv)
    transpose(xo, 3)
    multiply([(xr, 2), (xo, 3)])

    order = (y, left, right, opp)
    for q in (1, 2, 3, 0):
        g = dot(xt[...], pb[q])
        for a in range(4):
            for b in range(8):
                at = pl.ds(pl.multiple_of(order[a] * 64 + (b // 2) * 16, 16), 16)
                gst[b % 2, q, at, :] = g[a * 128 + b * 16 : a * 128 + b * 16 + 16]
        remote(gst.at[1 - core, q], d0.at[q], d_send.at[q], d_recv.at[q], (sib, y)).start()

    targets = {1: (left, 2), 2: (right, 1), 3: (opp, 3)}
    for q in (1, 2, 3):
        wait_bytes(d0.at[q], d_recv.at[q])
        hs[q - 1] = (gst[core, q] + d0[q]).astype(BF16)
        dev, lands = targets[q]
        remote(hs.at[q - 1], hr.at[lands - 1], h_send.at[q - 1], h_recv.at[lands - 1], (me, dev)).start()
    wait_bytes(d0.at[0], d_recv.at[0])
    total = gst[core, 0] + d0[0]
    for q in (1, 2, 3):
        wait_bytes(hr.at[q - 1], h_recv.at[q - 1])
        total = total + hr[q - 1].astype(F32)
    tot[...] = total.reshape(16, 16, 256)

    def send_tot(g, _):
        q = chip_at(g)
        remote(tot.at[q], tr.at[p], t_send, t_recv, (q * 2 + core, y)).start()
        return 0

    lax.fori_loop(1, 16, send_tot, 0)
    tr[p] = tot[p]
    wait_bytes(tr.at[pl.ds(0, 15)], t_recv)
    final = jnp.sum(tr[...], axis=0)
    stiff[...] = final[:, 0:128]
    mass[...] = final[:, 128:256]

    wait_bytes(send_m.at[pl.ds(0, 62)], sm_send)
    wait_bytes(send_r.at[pl.ds(0, 31 * 16)], sr_send)
    wait_bytes(x0, fr_send)
    wait_bytes(x0, fl_send)
    wait_bytes(lo, rr_send)
    wait_bytes(lo, rl_send)
    for q in range(4):
        wait_bytes(d0.at[q], d_send.at[q])
    for q in range(3):
        wait_bytes(hs.at[q], h_send.at[q])
    wait_bytes(tot.at[pl.ds(0, 15)], t_send)


def body(elem_records, elem_owner, elem_block, elem_offset, modes, mode_readers, pattern):
    lane = lax.broadcasted_iota(I32, (256, 128), 1)
    place = jnp.where(
        lane == 0, elem_block[:, None], jnp.where(lane == 1, elem_offset[:, None], 0)
    ).astype(BF16)
    flat = mode_readers.reshape(-1)
    ids = jnp.arange(32, dtype=I32)
    rank = jnp.sum(((flat[:, None] == flat[None, :]) & (ids[:, None] < ids[None, :])).astype(I32), axis=0)
    slot = flat * 2 + rank
    hit = slot[None, :] == jnp.arange(NQ, dtype=I32)[:, None]
    midx = jnp.sum(jnp.where(hit, ids[None, :] // 2 + 1, 0), axis=1) - 1
    dma = pltpu.SemaphoreType.DMA
    vm = pl.BlockSpec(memory_space=pltpu.VMEM)
    sm = pl.BlockSpec(memory_space=pltpu.SMEM)
    xbuf = pltpu.VMEM((NQ, BS, COLS), BF16)
    return pl.pallas_call(
        kernel,
        out_shape=(jax.ShapeDtypeStruct((16, 128), F32), jax.ShapeDtypeStruct((16, 128), F32)),
        in_specs=[sm, sm, vm, vm, vm, vm, vm],
        out_specs=(vm, vm),
        scratch_shapes=[
            xbuf, xbuf, xbuf, xbuf, xbuf,
            pltpu.VMEM((512, KA), BF16),
            pltpu.VMEM((512, KA), BF16),
            pltpu.VMEM((24, 256, 256), BF16),
            pltpu.VMEM((10, 256, KA), BF16),
            pltpu.VMEM((2, 128 * 64, 128), F32),
            pltpu.VMEM((64, 128, 256), BF16),
            pltpu.VMEM((512, 4096), BF16),
            pltpu.VMEM((4, 4096, 256), BF16),
            pltpu.VMEM((2, 4, 256, 256), F32),
            pltpu.VMEM((4, 256, 256), F32),
            pltpu.VMEM((3, 256, 256), BF16),
            pltpu.VMEM((3, 256, 256), BF16),
            pltpu.VMEM((16, 16, 256), F32),
            pltpu.VMEM((16, 16, 256), F32),
            dma, dma((16,)), dma, dma, dma, dma, dma((16,)), dma((16,)),
            dma, dma, dma, dma, dma((4,)), dma((4,)), dma((3,)), dma((3,)), dma, dma,
        ],
        compiler_params=pltpu.CompilerParams(
            collective_id=0, has_side_effects=True, vmem_limit_bytes=60 << 20
        ),
        name="sweep",
    )(midx, pattern.reshape(-1), elem_records, place, elem_owner.reshape(1, 256), elem_owner, modes)


def solution(mesh):
    in_specs = (
        P(("sub", "col"), None),
        P(("sub", "col"), None),
        P(("sub", "col")),
        P(("sub", "col")),
        P("sub", None, "col"),
        P("sub", None),
        P("sub", None),
    )
    out_specs = (P("sub", "col"), P("sub", "col"))
    return jax.shard_map(body, mesh=mesh, in_specs=in_specs, out_specs=out_specs, check_vma=False)
```

```python
import functools

import jax
import jax.numpy as jnp
from jax import lax
from jax.experimental import pallas as pl
from jax.experimental.pallas import tpu as pltpu
from jax.sharding import PartitionSpec as P

MESH = pl.DeviceIdType.MESH
BF16 = jnp.bfloat16
F32 = jnp.float32
I32 = jnp.int32

BS = 64
NQ = 64
NNZ = 4
KW = 1152
KA = 1280
COLS = 128
SLOTS_E = 16


def dot(a, b):
    return jnp.dot(a, b, preferred_element_type=F32)


def dot_nt(a, b):
    return lax.dot_general(a, b, (((1,), (1,)), ((), ())), preferred_element_type=F32)


FAR = (
    (2, 2), (2, 0), (0, 2), (3, 2), (2, 3), (1, 2), (2, 1), (3, 1),
    (1, 3), (3, 3), (1, 1), (3, 0), (0, 3), (1, 0), (0, 1),
)


def kernel(
    midx, pat, rec, place, owner_row, owner_col, modes,
    stiff, mass,
    send_m, xf, send_r, rbuf, ebuf, mbuf, ks, lb, xt, pb, gst, d0, hs, hr, tot, tr,
    sm_send, a_recv, r_send, r_recv, w_send, w_recv, b_send, b_recv, c_send, c_recv,
    e_send, e_recv, d_send, d_recv, h_send, h_recv, t_send, t_recv, patv, pats, p_send, p_recv, p_copy,
):
    me = lax.axis_index("sub")
    y = lax.axis_index("col")
    core = lax.rem(me, 2)
    p = me // 2
    z = p // 4
    x = lax.rem(p, 4)
    sib = p * 2 + 1 - core
    host = y // 2
    guest = lax.rem(core + host, 2)
    own = 4 * guest
    y1 = y + 1 - 2 * lax.rem(y, 2)
    y3 = 3 - y
    y2 = 3 - y1
    order = (y, y1, y3, y2)

    def chip_at(dz, dx):
        return lax.rem(z + dz, 4) * 4 + lax.rem(x + dx, 4)

    def remote(src, dst, ssem, rsem, dev):
        return pltpu.make_async_remote_copy(
            src_ref=src, dst_ref=dst, send_sem=ssem, recv_sem=rsem, device_id=dev, device_id_type=MESH
        )

    def wait_bytes(ref, sem):
        pltpu.make_async_copy(ref, ref, sem).wait()

    barrier = pltpu.get_barrier_semaphore()

    def hello(dev):
        pl.semaphore_signal(barrier, inc=1, device_id=dev, device_id_type=MESH)

    hello((sib, y))
    for yy in order[1:]:
        for cc in range(2):
            hello((p * 2 + cc, yy))

    def greet(g, _):
        q = chip_at(g // 4, lax.rem(g, 4))
        for cc in range(2):
            hello((q * 2 + cc, y))
        return 0

    lax.fori_loop(1, 16, greet, 0)

    @pl.when(guest == 1)
    def _():
        def greet_far(g, _):
            hello((g, y3))
            return 0

        lax.fori_loop(0, 32, greet_far, 0)

    def fill(s, _):
        k = midx[s]
        block = modes[jnp.maximum(k, 0)]
        send_m[s] = jnp.where(k >= 0, block, jnp.zeros_like(block))
        return 0

    lax.fori_loop(0, NQ, fill, 0, unroll=4)

    before = lax.broadcasted_iota(I32, (256, 256), 0) < lax.broadcasted_iota(I32, (256, 256), 1)
    same = owner_col[...] == owner_row[...]
    rank = jnp.sum(jnp.where(same & before, 1, 0), axis=0, keepdims=True)
    pos = owner_row[...] * SLOTS_E + rank

    def permute(g, _):
        rows = lax.broadcasted_iota(I32, (128, 256), 0) + g * 128
        pick = jnp.where(rows == pos, 1.0, 0.0).astype(BF16)
        at = pl.ds(pl.multiple_of(g * 128, 128), 128)
        send_r[at, 0:KW] = dot(pick, rec[...]).astype(BF16)
        send_r[at, KW:KA] = dot(pick, place[...]).astype(BF16)
        return 0

    lax.fori_loop(0, 4, permute, 0)

    pl.semaphore_wait(barrier, 53)

    xf[own, pl.ds(2 * me, 2)] = send_m[pl.ds(2 * me, 2)]

    @pl.when(guest == 0)
    def _():
        away = remote(pat, patv, p_send, p_recv, (sib, y))
        away.start()
        here = pltpu.make_async_copy(pat, pats, p_copy)
        here.start()
        away.wait_send()
        here.wait()

    def other(cc):
        return lax.rem(cc + host, 2)

    def send_mode(dest, lands):
        remote(
            send_m.at[pl.ds(2 * dest, 2)], xf.at[lands, pl.ds(2 * me, 2)], sm_send, a_recv.at[p], (dest, y)
        ).start()

    def rows16(n):
        return pl.ds(pl.multiple_of(n * 16, 16), 16)

    def send_rec(q, cc):
        far = other(cc)
        remote(
            send_r.at[rows16(q * 2 + cc)], rbuf.at[rows16(32 * far + me)], r_send, r_recv,
            (q * 2 + host, y + far * (y3 - y)),
        ).start()

    send_mode(sib, 4 * (1 - guest))
    for dz, dx in FAR:
        q = chip_at(dz, dx)
        for cc in range(2):
            send_mode(q * 2 + cc, 4 * other(cc))

    @pl.when(guest == 0)
    def _():
        rbuf[rows16(me)] = send_r[rows16(me)]

    for dz, dx in FAR:
        q = chip_at(dz, dx)
        for cc in range(2):
            send_rec(q, cc)
    remote(
        send_r.at[rows16(p * 2 + 1 - host)], rbuf.at[rows16(32 + me)], r_send, r_recv, (p * 2 + host, y3)
    ).start()

    @pl.when(guest == 1)
    def _():
        remote(send_r.at[rows16(sib)], rbuf.at[rows16(me)], r_send, r_recv, (sib, y)).start()

    def first(q, fresh):
        at = pl.ds(4 * q, 4)
        wait_bytes(fresh, a_recv.at[q])
        remote(
            xf.at[own, at], xf.at[1 + guest, at], b_send, b_recv.at[q],
            (me + guest * (sib - me), y1 + guest * (y3 - y1)),
        ).start()

        @pl.when(guest == 0)
        def _():
            remote(xf.at[0, at], xf.at[0, at], c_send, c_recv.at[0], (sib, y)).start()

    def second(q):
        at = pl.ds(4 * q, 4)
        wait_bytes(xf.at[1 + guest, at], b_recv.at[q])

        @pl.when(guest == 1)
        def _():
            remote(xf.at[2, at], xf.at[3, at], e_send, e_recv.at[q], (me, y1)).start()

        remote(xf.at[1 + guest, at], xf.at[1 + guest, at], c_send, c_recv.at[1 + guest], (sib, y)).start()

    def third(q):
        at = pl.ds(4 * q, 4)

        @pl.when(guest == 1)
        def _():
            wait_bytes(xf.at[3, at], e_recv.at[q])
            remote(xf.at[3, at], xf.at[3, at], c_send, c_recv.at[3], (sib, y)).start()

    chips = [p] + [chip_at((4 - dz) % 4, (4 - dx) % 4) for dz, dx in FAR]
    for n, q in enumerate(chips):
        first(q, xf.at[own, pl.ds(2 * sib, 2)] if n == 0 else xf.at[own, pl.ds(4 * q, 4)])

    def place_matrix(n, _):
        ri = n // 6
        o = lax.rem(n, 6)
        k = lax.broadcasted_iota(I32, (256, 256), 0)
        col = lax.broadcasted_iota(I32, (256, 256), 1)
        bb = (col & 63) - 8 * o
        hit = (k == 32 * ri + (col >> 6) * 24 + bb) & (bb >= 0) & (bb < 24)
        ebuf[n] = jnp.where(hit, 1.0, 0.0).astype(BF16)
        return 0

    lax.fori_loop(0, 24, place_matrix, 0)
    for o in (0, 1, 8, 9):
        mbuf[o] = jnp.zeros((128, KA), BF16)

    for q in chips:
        second(q)
    for q in chips:
        third(q)

    @pl.when(guest == 1)
    def _():
        wait_bytes(patv, p_recv)
        here = pltpu.make_async_copy(patv, pats, p_copy)
        here.start()
        here.wait()

    @pl.when(guest == 0)
    def _():
        wait_bytes(rbuf.at[pl.ds(0, 31 * 16)], r_recv)

    @pl.when(guest == 1)
    def _():
        wait_bytes(rbuf.at[pl.ds(0, 32 * 16)], r_recv)

    mine = pl.ds(pl.multiple_of(512 * guest, 512), 512)
    remote(rbuf.at[mine], rbuf.at[mine], w_send, w_recv, (sib, y)).start()
    wait_bytes(rbuf.at[pl.ds(pl.multiple_of(512 * (1 - guest), 512), 512)], w_recv)

    lane = lax.broadcasted_iota(I32, (8, 128), 1)
    rowi = lax.broadcasted_iota(I32, (8, 128), 0)
    pickrow = jnp.where(lane == rowi, 1.0, 0.0).astype(BF16)
    where = dot_nt(pickrow, rbuf[:, KW:KA]).astype(I32)
    blk = where[0:1]
    row = (blk >> 2) - 32 * core
    key = jnp.where((row >= 0) & (row < 32), where[1:2] * 128 + (blk & 3) * 32 + row, -1)

    def collect(o, _):
        rows = lax.broadcasted_iota(I32, (128, 1024), 0) + o * 128
        pick = jnp.where(rows == key, 1.0, 0.0).astype(BF16)
        mbuf[o + 2] = dot(pick, rbuf[...]).astype(BF16)
        return 0

    lax.fori_loop(0, 6, collect, 0)

    def assemble(v, _):
        for c in range(2):
            for w in range(2):
                acc = None
                for d in range(3):
                    start = c * 576 + 96 * (w + 2 * d)
                    base = start // 128 * 128
                    ri = (start - base) // 32
                    term = dot(
                        mbuf[v - d + 2, :, base : base + 256],
                        ebuf[ri * 6 + jnp.clip(v - d, 0, 5)],
                    )
                    acc = term if acc is None else acc + term
                acc = acc.astype(BF16)
                for a4 in range(4):
                    ks[c * 64 + 8 * v + 4 * w + a4] = jnp.concatenate(
                        [acc[j * 32 : j * 32 + 32, a4 * 64 : a4 * 64 + 64] for j in range(4)], axis=1
                    )
        return 0

    lax.fori_loop(0, 8, assemble, 0)

    r0 = lax.broadcasted_iota(I32, (256, 256), 0)
    r1 = lax.broadcasted_iota(I32, (256, 256), 1)
    swap = jnp.where((r0 >> 4 == (r1 & 15)) & ((r0 & 15) == r1 >> 4), 1.0, 0.0).astype(BF16)

    def turn(n, _):
        arow = pl.ds(pl.multiple_of(n // 2 * 16, 16), 16)
        irow = pl.ds(pl.multiple_of(lax.rem(n, 2) * 16, 16), 16)
        part = ks[arow, irow, :].reshape(256, 256)
        lb[irow, arow, :] = dot(swap, part).astype(BF16).reshape(16, 16, 256)
        return 0

    lax.fori_loop(0, 16, turn, 0, unroll=2)

    eye = jnp.where(
        lax.broadcasted_iota(I32, (128, 128), 0) == lax.broadcasted_iota(I32, (128, 128), 1), 1.0, 0.0
    ).astype(BF16)

    def transpose(k):
        def one(g, _):
            part = xf[k, pl.ds(32 * core + 4 * g, 4)].reshape(256, COLS)
            xt[k * 128 : k * 128 + 128, pl.ds(pl.multiple_of(g * 256, 256), 256)] = dot_nt(eye, part).astype(BF16)
            return 0

        lax.fori_loop(0, 8, one, 0, unroll=4)

    def multiply(kinds):
        def one(i, _):
            ids = [pats[core, 4 * i + j] for j in range(4)]
            right_side = jnp.concatenate(
                [jnp.concatenate([xf[k, n] for n in ids], axis=0) for k in kinds], axis=1
            )
            out = dot(lb[i], right_side).astype(BF16)
            at = pl.ds(pl.multiple_of(i * 64, 64), 64)
            for n, k in enumerate(kinds):
                pb[k, at, 0:128] = out[0:64, n * 128 : n * 128 + 128]
                pb[k, at, 128:256] = out[64:128, n * 128 : n * 128 + 128]
            return 0

        lax.fori_loop(0, 32, one, 0, unroll=4)

    @pl.when(guest == 0)
    def _():
        wait_bytes(xf.at[2], c_recv.at[2])
        wait_bytes(xf.at[3], c_recv.at[3])

    @pl.when(guest == 1)
    def _():
        wait_bytes(xf.at[0], c_recv.at[0])
        wait_bytes(xf.at[1], c_recv.at[1])

    for k in range(4):
        transpose(k)
    multiply((0, 1))
    multiply((2, 3))

    for q in (3, 2, 1, 0):
        g = dot(xt[...], pb[q])
        for a in range(4):
            for b in range(8):
                at = pl.ds(pl.multiple_of(order[a] * 64 + (b // 2) * 16, 16), 16)
                gst[b % 2, q, at, :] = g[a * 128 + b * 16 : a * 128 + b * 16 + 16]
        remote(gst.at[1 - core, q], d0.at[q], d_send.at[q], d_recv.at[q], (sib, y)).start()

    for q in (3, 2, 1):
        wait_bytes(d0.at[q], d_recv.at[q])
        hs[q - 1] = (gst[core, q] + d0[q]).astype(BF16)
        remote(hs.at[q - 1], hr.at[y], h_send.at[q - 1], h_recv.at[y], (me, order[q])).start()
    wait_bytes(d0.at[0], d_recv.at[0])
    total = gst[core, 0] + d0[0]
    for yy in (y2, y3, y1):
        wait_bytes(hr.at[yy], h_recv.at[yy])
        total = total + hr[yy].astype(F32)
    tot[...] = total.reshape(16, 16, 256)

    for dz, dx in FAR:
        q = chip_at(dz, dx)
        remote(tot.at[q], tr.at[p], t_send, t_recv, (q * 2 + core, y)).start()
    tr[p] = tot[p]
    wait_bytes(tr.at[pl.ds(0, 15)], t_recv)
    final = jnp.sum(tr[...], axis=0)
    stiff[...] = final[:, 0:128]
    mass[...] = final[:, 128:256]

    wait_bytes(send_m.at[pl.ds(0, 62)], sm_send)
    wait_bytes(rbuf.at[mine], w_send)
    wait_bytes(xf.at[0], b_send)
    wait_bytes(xf.at[pl.ds(0, 2)], c_send)

    @pl.when(guest == 0)
    def _():
        wait_bytes(send_r.at[pl.ds(0, 31 * 16)], r_send)

    @pl.when(guest == 1)
    def _():
        wait_bytes(send_r, r_send)
        wait_bytes(xf.at[0], e_send)

    for q in range(4):
        wait_bytes(d0.at[q], d_send.at[q])
    for q in range(3):
        wait_bytes(hs.at[q], h_send.at[q])
    wait_bytes(tot.at[pl.ds(0, 15)], t_send)


def body(elem_records, elem_owner, elem_block, elem_offset, modes, mode_readers, pattern):
    lane = lax.broadcasted_iota(I32, (256, 128), 1)
    place = jnp.where(
        lane == 0, elem_block[:, None], jnp.where(lane == 1, elem_offset[:, None], 0)
    ).astype(BF16)
    flat = mode_readers.reshape(-1)
    ids = jnp.arange(32, dtype=I32)
    rank = jnp.sum(((flat[:, None] == flat[None, :]) & (ids[:, None] < ids[None, :])).astype(I32), axis=0)
    slot = flat * 2 + rank
    hit = slot[None, :] == jnp.arange(NQ, dtype=I32)[:, None]
    midx = jnp.sum(jnp.where(hit, ids[None, :] // 2 + 1, 0), axis=1) - 1
    dma = pltpu.SemaphoreType.DMA
    vm = pl.BlockSpec(memory_space=pltpu.VMEM)
    sm = pl.BlockSpec(memory_space=pltpu.SMEM)
    return pl.pallas_call(
        kernel,
        out_shape=(jax.ShapeDtypeStruct((16, 128), F32), jax.ShapeDtypeStruct((16, 128), F32)),
        in_specs=[sm, vm, vm, vm, vm, vm, vm],
        out_specs=(vm, vm),
        scratch_shapes=[
            pltpu.VMEM((NQ, BS, COLS), BF16),
            pltpu.VMEM((5, NQ, BS, COLS), BF16),
            pltpu.VMEM((512, KA), BF16),
            pltpu.VMEM((1024, KA), BF16),
            pltpu.VMEM((24, 256, 256), BF16),
            pltpu.VMEM((10, 128, KA), BF16),
            pltpu.VMEM((128, 32, 256), BF16),
            pltpu.VMEM((32, 128, 256), BF16),
            pltpu.VMEM((512, 2048), BF16),
            pltpu.VMEM((4, 2048, 256), BF16),
            pltpu.VMEM((2, 4, 256, 256), F32),
            pltpu.VMEM((4, 256, 256), F32),
            pltpu.VMEM((3, 256, 256), BF16),
            pltpu.VMEM((4, 256, 256), BF16),
            pltpu.VMEM((16, 16, 256), F32),
            pltpu.VMEM((16, 16, 256), F32),
            dma, dma((16,)), dma, dma, dma, dma, dma, dma((16,)), dma, dma((4,)),
            dma, dma((16,)), dma((4,)), dma((4,)), dma((3,)), dma((4,)), dma, dma,
            pltpu.VMEM((2, 128), I32), pltpu.SMEM((2, 128), I32), dma, dma, dma,
        ],
        compiler_params=pltpu.CompilerParams(
            collective_id=0, has_side_effects=True, vmem_limit_bytes=60 << 20
        ),
        name="sweep",
    )(midx, pattern.reshape(2, 128), elem_records, place, elem_owner.reshape(1, 256), elem_owner, modes)


def solution(mesh):
    in_specs = (
        P(("sub", "col"), None),
        P(("sub", "col"), None),
        P(("sub", "col")),
        P(("sub", "col")),
        P("sub", None, "col"),
        P("sub", None),
        P("sub", None),
    )
    out_specs = (P("sub", "col"), P("sub", "col"))
    return jax.shard_map(body, mesh=mesh, in_specs=in_specs, out_specs=out_specs, check_vma=False)
```

```python
import functools

import jax
import jax.numpy as jnp
from jax import lax
from jax.experimental import pallas as pl
from jax.experimental.pallas import tpu as pltpu
from jax.sharding import PartitionSpec as P

MESH = pl.DeviceIdType.MESH
BF16 = jnp.bfloat16
F32 = jnp.float32
I32 = jnp.int32

BS = 64
NQ = 64
NNZ = 4
KW = 1152
KA = 1280
COLS = 128
SLOTS_E = 16


def dot(a, b):
    return jnp.dot(a, b, preferred_element_type=F32)


def dot_nt(a, b):
    return lax.dot_general(a, b, (((1,), (1,)), ((), ())), preferred_element_type=F32)


FAR = (
    (2, 2), (2, 0), (0, 2), (3, 2), (2, 3), (1, 2), (2, 1), (3, 1),
    (1, 3), (3, 3), (1, 1), (3, 0), (0, 3), (1, 0), (0, 1),
)


def kernel(
    pat, rec, owner_row, block_row, offset_row, modes, readers,
    out,
    send_m, xf, send_r, rbuf, ebuf, mbuf, ks, lb, xt, pb, gst, d0, hs, hr, tot, tr,
    sm_send, a_recv, r_send, r_recv, w_send, w_recv, b_send, b_recv, c_send, c_recv,
    e_send, e_recv, d_send, d_recv, h_send, h_recv, t_send, t_recv, tab, patv, pats, mids, p_send, p_recv, p_copy, m_copy,
):
    me = lax.axis_index("sub")
    y = lax.axis_index("col")
    core = lax.rem(me, 2)
    p = me // 2
    z = p // 4
    x = lax.rem(p, 4)
    sib = p * 2 + 1 - core
    host = y // 2
    guest = lax.rem(core + host, 2)
    own = 4 * guest
    y1 = y + 1 - 2 * lax.rem(y, 2)
    y3 = 3 - y
    y2 = 3 - y1
    order = (y, y1, y3, y2)

    def chip_at(dz, dx):
        return lax.rem(z + dz, 4) * 4 + lax.rem(x + dx, 4)

    def remote(src, dst, ssem, rsem, dev):
        return pltpu.make_async_remote_copy(
            src_ref=src, dst_ref=dst, send_sem=ssem, recv_sem=rsem, device_id=dev, device_id_type=MESH
        )

    def wait_bytes(ref, sem):
        pltpu.make_async_copy(ref, ref, sem).wait()

    barrier = pltpu.get_barrier_semaphore()

    def hello(dev):
        pl.semaphore_signal(barrier, inc=1, device_id=dev, device_id_type=MESH)

    hello((sib, y))
    for yy in order[1:]:
        for cc in range(2):
            hello((p * 2 + cc, yy))

    def greet(g, _):
        q = chip_at(g // 4, lax.rem(g, 4))
        for cc in range(2):
            hello((q * 2 + cc, y))
        return 0

    lax.fori_loop(1, 16, greet, 0)

    @pl.when(guest == 1)
    def _():
        def greet_far(g, _):
            hello((g, y3))
            return 0

        lax.fori_loop(0, 32, greet_far, 0)

    def iota(shape, axis):
        return lax.broadcasted_iota(I32, shape, axis)

    def eye(n):
        return jnp.where(iota((n, n), 0) == iota((n, n), 1), 1.0, 0.0).astype(BF16)

    named = dot_nt(eye(16), readers[...].astype(F32).astype(BF16))
    subs = iota((16, 32), 1).astype(F32)
    occurs = jnp.where((named[:, 0:1] == subs) | (named[:, 1:2] == subs), 1.0, 0.0)
    lower = jnp.where(iota((16, 16), 0) > iota((16, 16), 1), 1.0, 0.0).astype(BF16)
    ahead = dot(lower, occurs.astype(BF16))
    number = (iota((16, 32), 0) + 1).astype(F32)
    tab[...] = jnp.zeros((8, 128), I32)
    tab[0:4, 0:64] = pat[...]
    for n in range(2):
        picked = jnp.sum(jnp.where((occurs > 0) & (ahead == n), number, 0.0), axis=0, keepdims=True)
        tab[4 + n : 5 + n, 0:32] = picked.astype(I32) - 1
    to_mids = pltpu.make_async_copy(tab, mids, m_copy)
    to_mids.start()

    lines = iota((128, 256), 0)
    facts = jnp.where(
        lines == 0, block_row[...], jnp.where(lines == 1, offset_row[...], jnp.where(lines == 2, owner_row[...], 0))
    ).astype(F32).astype(BF16)
    place = dot_nt(eye(256), facts)
    before = iota((256, 256), 0) < iota((256, 256), 1)
    same = place[:, 2:3] == owner_row[...].astype(F32)
    rank = jnp.sum(jnp.where(same & before, 1, 0), axis=0, keepdims=True)
    pos = owner_row[...] * SLOTS_E + rank
    place = place.astype(BF16)

    def permute(g, _):
        pick = jnp.where(iota((128, 256), 0) + g * 128 == pos, 1.0, 0.0).astype(BF16)
        at = pl.ds(pl.multiple_of(g * 128, 128), 128)
        send_r[at, 0:KW] = dot(pick, rec[...]).astype(BF16)
        send_r[at, KW:KA] = dot(pick, place).astype(BF16)
        return 0

    lax.fori_loop(0, 4, permute, 0)

    to_mids.wait()

    def fill(s, _):
        k = mids[4 + lax.rem(s, 2), s // 2]
        block = modes[jnp.clip(k, 0, modes.shape[0] - 1)]
        send_m[s] = jnp.where(k >= 0, block, jnp.zeros_like(block))
        return 0

    lax.fori_loop(0, NQ, fill, 0, unroll=4)

    pl.semaphore_wait(barrier, 53)

    xf[own, pl.ds(2 * me, 2)] = send_m[pl.ds(2 * me, 2)]

    @pl.when(guest == 0)
    def _():
        away = remote(tab, patv, p_send, p_recv, (sib, y))
        away.start()
        here = pltpu.make_async_copy(tab, pats, p_copy)
        here.start()
        away.wait_send()
        here.wait()

    def other(cc):
        return lax.rem(cc + host, 2)

    def send_mode(dest, lands):
        remote(
            send_m.at[pl.ds(2 * dest, 2)], xf.at[lands, pl.ds(2 * me, 2)], sm_send, a_recv.at[p], (dest, y)
        ).start()

    def rows16(n):
        return pl.ds(pl.multiple_of(n * 16, 16), 16)

    def send_rec(q, cc):
        far = other(cc)
        remote(
            send_r.at[rows16(q * 2 + cc)], rbuf.at[rows16(32 * far + me)], r_send, r_recv,
            (q * 2 + host, y + far * (y3 - y)),
        ).start()

    send_mode(sib, 4 * (1 - guest))
    for dz, dx in FAR:
        q = chip_at(dz, dx)
        for cc in range(2):
            send_mode(q * 2 + cc, 4 * other(cc))

    @pl.when(guest == 0)
    def _():
        rbuf[rows16(me)] = send_r[rows16(me)]

    remote(
        send_r.at[rows16(p * 2 + 1 - host)], rbuf.at[rows16(32 + me)], r_send, r_recv, (p * 2 + host, y3)
    ).start()

    @pl.when(guest == 1)
    def _():
        remote(send_r.at[rows16(sib)], rbuf.at[rows16(me)], r_send, r_recv, (sib, y)).start()

    def first(q, fresh):
        at = pl.ds(4 * q, 4)
        wait_bytes(fresh, a_recv.at[q])
        remote(
            xf.at[own, at], xf.at[1 + guest, at], b_send, b_recv.at[q],
            (me + guest * (sib - me), y1 + guest * (y3 - y1)),
        ).start()

        @pl.when(guest == 0)
        def _():
            remote(xf.at[0, at], xf.at[0, at], c_send, c_recv.at[0], (sib, y)).start()

    def second(q):
        at = pl.ds(4 * q, 4)
        wait_bytes(xf.at[1 + guest, at], b_recv.at[q])

        @pl.when(guest == 1)
        def _():
            remote(xf.at[2, at], xf.at[3, at], e_send, e_recv.at[q], (me, y1)).start()

        remote(xf.at[1 + guest, at], xf.at[1 + guest, at], c_send, c_recv.at[1 + guest], (sib, y)).start()

    def third(q):
        at = pl.ds(4 * q, 4)

        @pl.when(guest == 1)
        def _():
            wait_bytes(xf.at[3, at], e_recv.at[q])
            remote(xf.at[3, at], xf.at[3, at], c_send, c_recv.at[3], (sib, y)).start()

    chips = [p] + [chip_at((4 - dz) % 4, (4 - dx) % 4) for dz, dx in FAR]
    for n, q in enumerate(chips):
        first(q, xf.at[own, pl.ds(2 * sib, 2)] if n == 0 else xf.at[own, pl.ds(4 * q, 4)])
    for dz, dx in FAR:
        for cc in range(2):
            send_rec(chip_at(dz, dx), cc)

    def place_matrix(n, _):
        ri = n // 6
        o = lax.rem(n, 6)
        k = lax.broadcasted_iota(I32, (256, 256), 0)
        col = lax.broadcasted_iota(I32, (256, 256), 1)
        bb = (col & 63) - 8 * o
        hit = (k == 32 * ri + (col >> 6) * 24 + bb) & (bb >= 0) & (bb < 24)
        ebuf[n] = jnp.where(hit, 1.0, 0.0).astype(BF16)
        return 0

    lax.fori_loop(0, 24, place_matrix, 0)
    for o in (0, 1, 8, 9):
        mbuf[o] = jnp.zeros((128, KA), BF16)

    for q in chips:
        second(q)
    for q in chips:
        third(q)

    @pl.when(guest == 1)
    def _():
        wait_bytes(patv, p_recv)
        here = pltpu.make_async_copy(patv, pats, p_copy)
        here.start()
        here.wait()

    turned = eye(128)

    def transpose(k):
        def one(g, _):
            part = xf[k, pl.ds(32 * core + 4 * g, 4)].reshape(256, COLS)
            xt[k * 128 : k * 128 + 128, pl.ds(pl.multiple_of(g * 256, 256), 256)] = dot_nt(turned, part).astype(BF16)
            return 0

        lax.fori_loop(0, 8, one, 0, unroll=4)

    @pl.when(guest == 0)
    def _():
        wait_bytes(xf.at[2], c_recv.at[2])
        wait_bytes(xf.at[3], c_recv.at[3])

    @pl.when(guest == 1)
    def _():
        wait_bytes(xf.at[0], c_recv.at[0])
        wait_bytes(xf.at[1], c_recv.at[1])

    for k in range(4):
        transpose(k)

    @pl.when(guest == 0)
    def _():
        wait_bytes(rbuf.at[pl.ds(0, 31 * 16)], r_recv)

    @pl.when(guest == 1)
    def _():
        wait_bytes(rbuf.at[pl.ds(0, 32 * 16)], r_recv)

    mine = pl.ds(pl.multiple_of(512 * guest, 512), 512)
    remote(rbuf.at[mine], rbuf.at[mine], w_send, w_recv, (sib, y)).start()
    wait_bytes(rbuf.at[pl.ds(pl.multiple_of(512 * (1 - guest), 512), 512)], w_recv)

    lane = lax.broadcasted_iota(I32, (8, 128), 1)
    rowi = lax.broadcasted_iota(I32, (8, 128), 0)
    pickrow = jnp.where(lane == rowi, 1.0, 0.0).astype(BF16)
    where = dot_nt(pickrow, rbuf[:, KW:KA]).astype(I32)
    blk = where[0:1]
    row = (blk >> 2) - 32 * core
    key = jnp.where((row >= 0) & (row < 32), where[1:2] * 128 + (blk & 3) * 32 + row, -1)

    def collect(o, _):
        rows = lax.broadcasted_iota(I32, (128, 1024), 0) + o * 128
        pick = jnp.where(rows == key, 1.0, 0.0).astype(BF16)
        mbuf[o + 2] = dot(pick, rbuf[...]).astype(BF16)
        return 0

    lax.fori_loop(0, 6, collect, 0)

    def assemble(v, _):
        for c in range(2):
            for w in range(2):
                acc = None
                for d in range(3):
                    start = c * 576 + 96 * (w + 2 * d)
                    base = start // 128 * 128
                    ri = (start - base) // 32
                    term = dot(
                        mbuf[v - d + 2, :, base : base + 256],
                        ebuf[ri * 6 + jnp.clip(v - d, 0, 5)],
                    )
                    acc = term if acc is None else acc + term
                acc = acc.astype(BF16)
                for a4 in range(4):
                    ks[c * 64 + 8 * v + 4 * w + a4] = jnp.concatenate(
                        [acc[j * 32 : j * 32 + 32, a4 * 64 : a4 * 64 + 64] for j in range(4)], axis=1
                    )
        return 0

    lax.fori_loop(0, 8, assemble, 0)

    r0 = lax.broadcasted_iota(I32, (256, 256), 0)
    r1 = lax.broadcasted_iota(I32, (256, 256), 1)
    swap = jnp.where((r0 >> 4 == (r1 & 15)) & ((r0 & 15) == r1 >> 4), 1.0, 0.0).astype(BF16)

    def turn(n, _):
        arow = pl.ds(pl.multiple_of(n // 2 * 16, 16), 16)
        irow = pl.ds(pl.multiple_of(lax.rem(n, 2) * 16, 16), 16)
        part = ks[arow, irow, :].reshape(256, 256)
        lb[irow, arow, :] = dot(swap, part).astype(BF16).reshape(16, 16, 256)
        return 0

    lax.fori_loop(0, 16, turn, 0, unroll=2)

    def multiply(kinds):
        def one(i, _):
            ids = [pats[j, 32 * core + i] for j in range(4)]
            right_side = jnp.concatenate(
                [jnp.concatenate([xf[k, n] for n in ids], axis=0) for k in kinds], axis=1
            )
            out = dot(lb[i], right_side).astype(BF16)
            at = pl.ds(pl.multiple_of(i * 64, 64), 64)
            for n, k in enumerate(kinds):
                pb[k, at, 0:128] = out[0:64, n * 128 : n * 128 + 128]
                pb[k, at, 128:256] = out[64:128, n * 128 : n * 128 + 128]
            return 0

        lax.fori_loop(0, 32, one, 0, unroll=4)

    def gram(q):
        g = dot(xt[...], pb[q])
        for a in range(4):
            for b in range(8):
                at = pl.ds(pl.multiple_of(order[a] * 64 + (b // 2) * 16, 16), 16)
                gst[b % 2, q, at, :] = g[a * 128 + b * 16 : a * 128 + b * 16 + 16]
        remote(gst.at[1 - core, q], d0.at[q], d_send.at[q], d_recv.at[q], (sib, y)).start()

    def pair_sum(q):
        wait_bytes(d0.at[q], d_recv.at[q])
        hs[q - 1] = (gst[core, q] + d0[q]).astype(BF16)
        remote(hs.at[q - 1], hr.at[y], h_send.at[q - 1], h_recv.at[y], (me, order[q])).start()

    multiply((2, 3))
    gram(3)
    gram(2)
    pair_sum(3)
    multiply((0, 1))
    pair_sum(2)
    gram(1)
    gram(0)
    pair_sum(1)
    wait_bytes(d0.at[0], d_recv.at[0])
    total = gst[core, 0] + d0[0]
    for yy in (y2, y3, y1):
        wait_bytes(hr.at[yy], h_recv.at[yy])
        total = total + hr[yy].astype(F32)
    tot[...] = total.reshape(16, 16, 256)

    for dz, dx in FAR:
        q = chip_at(dz, dx)
        remote(tot.at[q], tr.at[p], t_send, t_recv, (q * 2 + core, y)).start()
    tr[p] = tot[p]
    wait_bytes(tr.at[pl.ds(0, 15)], t_recv)
    out[...] = jnp.sum(tr[...], axis=0)

    wait_bytes(send_m.at[pl.ds(0, 62)], sm_send)
    wait_bytes(rbuf.at[mine], w_send)
    wait_bytes(xf.at[0], b_send)
    wait_bytes(xf.at[pl.ds(0, 2)], c_send)

    @pl.when(guest == 0)
    def _():
        wait_bytes(send_r.at[pl.ds(0, 31 * 16)], r_send)

    @pl.when(guest == 1)
    def _():
        wait_bytes(send_r, r_send)
        wait_bytes(xf.at[0], e_send)

    for q in range(4):
        wait_bytes(d0.at[q], d_send.at[q])
    for q in range(3):
        wait_bytes(hs.at[q], h_send.at[q])
    wait_bytes(tot.at[pl.ds(0, 15)], t_send)


def body(elem_records, elem_owner, elem_block, elem_offset, modes, mode_readers, pattern):
    dma = pltpu.SemaphoreType.DMA
    vm = pl.BlockSpec(memory_space=pltpu.VMEM)
    out = pl.pallas_call(
        kernel,
        out_shape=jax.ShapeDtypeStruct((16, 256), F32),
        in_specs=[vm] * 7,
        out_specs=vm,
        scratch_shapes=[
            pltpu.VMEM((NQ, BS, COLS), BF16),
            pltpu.VMEM((5, NQ, BS, COLS), BF16),
            pltpu.VMEM((512, KA), BF16),
            pltpu.VMEM((1024, KA), BF16),
            pltpu.VMEM((24, 256, 256), BF16),
            pltpu.VMEM((10, 128, KA), BF16),
            pltpu.VMEM((128, 32, 256), BF16),
            pltpu.VMEM((32, 128, 256), BF16),
            pltpu.VMEM((512, 2048), BF16),
            pltpu.VMEM((4, 2048, 256), BF16),
            pltpu.VMEM((2, 4, 256, 256), F32),
            pltpu.VMEM((4, 256, 256), F32),
            pltpu.VMEM((3, 256, 256), BF16),
            pltpu.VMEM((4, 256, 256), BF16),
            pltpu.VMEM((16, 16, 256), F32),
            pltpu.VMEM((16, 16, 256), F32),
            dma, dma((16,)), dma, dma, dma, dma, dma, dma((16,)), dma, dma((4,)),
            dma, dma((16,)), dma((4,)), dma((4,)), dma((3,)), dma((4,)), dma, dma,
            pltpu.VMEM((8, 128), I32), pltpu.VMEM((8, 128), I32), pltpu.SMEM((8, 128), I32), pltpu.SMEM((8, 128), I32),
            dma, dma, dma, dma,
        ],
        compiler_params=pltpu.CompilerParams(
            collective_id=0, has_side_effects=True, vmem_limit_bytes=60 << 20
        ),
        name="sweep",
    )(
        pattern.T, elem_records, elem_owner.T, elem_block.reshape(1, 256), elem_offset.reshape(1, 256),
        modes, mode_readers.T,
    )
    return out[:, 0:128], out[:, 128:256]


def solution(mesh):
    in_specs = (
        P(("sub", "col"), None),
        P(("sub", "col"), None),
        P(("sub", "col")),
        P(("sub", "col")),
        P("sub", None, "col"),
        P("sub", None),
        P("sub", None),
    )
    out_specs = (P("sub", "col"), P("sub", "col"))
    return jax.shard_map(body, mesh=mesh, in_specs=in_specs, out_specs=out_specs, check_vma=False)
```

```python
import functools

import jax
import jax.numpy as jnp
from jax import lax
from jax.experimental import pallas as pl
from jax.experimental.pallas import tpu as pltpu
from jax.sharding import PartitionSpec as P

MESH = pl.DeviceIdType.MESH
BF16 = jnp.bfloat16
F32 = jnp.float32
I32 = jnp.int32

BS = 64
NQ = 64
NNZ = 4
KW = 1152
KA = 1280
COLS = 128
SLOTS_E = 16


def dot(a, b):
    return jnp.dot(a, b, preferred_element_type=F32)


def dot_nt(a, b):
    return lax.dot_general(a, b, (((1,), (1,)), ((), ())), preferred_element_type=F32)


FAR = (
    (2, 2), (2, 0), (0, 2), (3, 2), (2, 3), (1, 2), (2, 1), (3, 1),
    (1, 3), (3, 3), (1, 1), (3, 0), (0, 3), (1, 0), (0, 1),
)


def kernel(
    pat, rec, owner_row, block_row, offset_row, modes, readers,
    out,
    send_m, xf, send_r, rbuf, ebuf, mbuf, ks, lb, xt, pb, gst, d0, hs, hr, tot, tr,
    sm_send, a_recv, r_send, r_recv, w_send, w_recv, b_send, b_recv, c_send, c_recv,
    e_send, e_recv, d_send, d_recv, h_send, h_recv, t_send, t_recv, tab, patv, pats, mids, p_send, p_recv, p_copy, m_copy,
):
    me = lax.axis_index("sub")
    y = lax.axis_index("col")
    core = lax.rem(me, 2)
    p = me // 2
    z = p // 4
    x = lax.rem(p, 4)
    sib = p * 2 + 1 - core
    host = y // 2
    guest = lax.rem(core + host, 2)
    own = 4 * guest
    y1 = y + 1 - 2 * lax.rem(y, 2)
    y3 = 3 - y
    y2 = 3 - y1
    order = (y, y1, y3, y2)

    def chip_at(dz, dx):
        return lax.rem(z + dz, 4) * 4 + lax.rem(x + dx, 4)

    def remote(src, dst, ssem, rsem, dev):
        return pltpu.make_async_remote_copy(
            src_ref=src, dst_ref=dst, send_sem=ssem, recv_sem=rsem, device_id=dev, device_id_type=MESH
        )

    def wait_bytes(ref, sem):
        pltpu.make_async_copy(ref, ref, sem).wait()

    barrier = pltpu.get_barrier_semaphore()

    def hello(dev):
        pl.semaphore_signal(barrier, inc=1, device_id=dev, device_id_type=MESH)

    hello((sib, y))
    for yy in order[1:]:
        for cc in range(2):
            hello((p * 2 + cc, yy))

    def greet(g, _):
        q = chip_at(g // 4, lax.rem(g, 4))
        for cc in range(2):
            hello((q * 2 + cc, y))
        return 0

    lax.fori_loop(1, 16, greet, 0)

    @pl.when(guest == 1)
    def _():
        def greet_far(g, _):
            hello((g, y3))
            return 0

        lax.fori_loop(0, 32, greet_far, 0)

    def iota(shape, axis):
        return lax.broadcasted_iota(I32, shape, axis)

    def eye(n):
        return jnp.where(iota((n, n), 0) == iota((n, n), 1), 1.0, 0.0).astype(BF16)

    named = dot_nt(eye(16), readers[...].astype(F32).astype(BF16))
    subs = iota((16, 32), 1).astype(F32)
    occurs = jnp.where((named[:, 0:1] == subs) | (named[:, 1:2] == subs), 1.0, 0.0)
    lower = jnp.where(iota((16, 16), 0) > iota((16, 16), 1), 1.0, 0.0).astype(BF16)
    ahead = dot(lower, occurs.astype(BF16))
    number = (iota((16, 32), 0) + 1).astype(F32)
    tab[...] = jnp.zeros((8, 128), I32)
    tab[0:4, 0:64] = pat[...]
    for n in range(2):
        picked = jnp.sum(jnp.where((occurs > 0) & (ahead == n), number, 0.0), axis=0, keepdims=True)
        tab[4 + n : 5 + n, 0:32] = picked.astype(I32) - 1
    to_mids = pltpu.make_async_copy(tab, mids, m_copy)
    to_mids.start()

    lines = iota((128, 256), 0)
    facts = jnp.where(
        lines == 0, block_row[...], jnp.where(lines == 1, offset_row[...], jnp.where(lines == 2, owner_row[...], 0))
    ).astype(F32).astype(BF16)
    place = dot_nt(eye(256), facts)
    before = iota((256, 256), 0) < iota((256, 256), 1)
    same = place[:, 2:3] == owner_row[...].astype(F32)
    rank = jnp.sum(jnp.where(same & before, 1, 0), axis=0, keepdims=True)
    pos = owner_row[...] * SLOTS_E + rank
    place = place.astype(BF16)

    def permute(g, _):
        pick = jnp.where(iota((128, 256), 0) + g * 128 == pos, 1.0, 0.0).astype(BF16)
        at = pl.ds(pl.multiple_of(g * 128, 128), 128)
        send_r[at, 0:KW] = dot(pick, rec[...]).astype(BF16)
        send_r[at, KW:KA] = dot(pick, place).astype(BF16)
        return 0

    lax.fori_loop(0, 4, permute, 0)

    to_mids.wait()

    def fill(s, _):
        k = mids[4 + lax.rem(s, 2), s // 2]
        block = modes[jnp.clip(k, 0, modes.shape[0] - 1)]
        send_m[s] = jnp.where(k >= 0, block, jnp.zeros_like(block))
        return 0

    lax.fori_loop(0, NQ, fill, 0, unroll=4)

    pl.semaphore_wait(barrier, 53)

    xf[own, pl.ds(2 * me, 2)] = send_m[pl.ds(2 * me, 2)]

    @pl.when(guest == 0)
    def _():
        away = remote(tab, patv, p_send, p_recv, (sib, y))
        away.start()
        here = pltpu.make_async_copy(tab, pats, p_copy)
        here.start()
        away.wait_send()
        here.wait()

    def other(cc):
        return lax.rem(cc + host, 2)

    def send_mode(dest, lands):
        remote(
            send_m.at[pl.ds(2 * dest, 2)], xf.at[lands, pl.ds(2 * me, 2)], sm_send, a_recv.at[p], (dest, y)
        ).start()

    def rows16(n):
        return pl.ds(pl.multiple_of(n * 16, 16), 16)

    def send_rec(q, cc):
        far = other(cc)
        remote(
            send_r.at[rows16(q * 2 + cc)], rbuf.at[rows16(32 * far + me)], r_send, r_recv,
            (q * 2 + host, y + far * (y3 - y)),
        ).start()

    send_mode(sib, 4 * (1 - guest))
    for dz, dx in FAR:
        q = chip_at(dz, dx)
        for cc in range(2):
            send_mode(q * 2 + cc, 4 * other(cc))

    @pl.when(guest == 0)
    def _():
        rbuf[rows16(me)] = send_r[rows16(me)]

    remote(
        send_r.at[rows16(p * 2 + 1 - host)], rbuf.at[rows16(32 + me)], r_send, r_recv, (p * 2 + host, y3)
    ).start()

    @pl.when(guest == 1)
    def _():
        remote(send_r.at[rows16(sib)], rbuf.at[rows16(me)], r_send, r_recv, (sib, y)).start()

    def first(q, fresh):
        at = pl.ds(4 * q, 4)
        wait_bytes(fresh, a_recv.at[q])
        remote(
            xf.at[own, at], xf.at[1 + guest, at], b_send, b_recv.at[q],
            (me + guest * (sib - me), y1 + guest * (y3 - y1)),
        ).start()

        @pl.when(guest == 0)
        def _():
            remote(xf.at[0, at], xf.at[0, at], c_send, c_recv.at[0], (sib, y)).start()

    def second(q):
        at = pl.ds(4 * q, 4)
        wait_bytes(xf.at[1 + guest, at], b_recv.at[q])

        @pl.when(guest == 1)
        def _():
            remote(xf.at[2, at], xf.at[3, at], e_send, e_recv.at[q], (me, y1)).start()

        remote(xf.at[1 + guest, at], xf.at[1 + guest, at], c_send, c_recv.at[1 + guest], (sib, y)).start()

    def third(q):
        at = pl.ds(4 * q, 4)

        @pl.when(guest == 1)
        def _():
            wait_bytes(xf.at[3, at], e_recv.at[q])
            remote(xf.at[3, at], xf.at[3, at], c_send, c_recv.at[3], (sib, y)).start()

    chips = [p] + [chip_at((4 - dz) % 4, (4 - dx) % 4) for dz, dx in FAR]
    for n, q in enumerate(chips):
        first(q, xf.at[own, pl.ds(2 * sib, 2)] if n == 0 else xf.at[own, pl.ds(4 * q, 4)])
    for cc in (host, 1 - host):
        for dz, dx in FAR:
            send_rec(chip_at(dz, dx), cc)

    def place_matrix(n, _):
        ri = n // 6
        o = lax.rem(n, 6)
        k = lax.broadcasted_iota(I32, (256, 256), 0)
        col = lax.broadcasted_iota(I32, (256, 256), 1)
        bb = (col & 63) - 8 * o
        hit = (k == 32 * ri + (col >> 6) * 24 + bb) & (bb >= 0) & (bb < 24)
        ebuf[n] = jnp.where(hit, 1.0, 0.0).astype(BF16)
        return 0

    lax.fori_loop(0, 24, place_matrix, 0)

    for q in chips:
        second(q)
    for q in chips:
        third(q)

    @pl.when(guest == 1)
    def _():
        wait_bytes(patv, p_recv)
        here = pltpu.make_async_copy(patv, pats, p_copy)
        here.start()
        here.wait()

    turned = eye(128)

    def transpose(k):
        def one(g, _):
            part = xf[k, pl.ds(32 * core + 4 * g, 4)].reshape(256, COLS)
            xt[k * 128 : k * 128 + 128, pl.ds(pl.multiple_of(g * 256, 256), 256)] = dot_nt(turned, part).astype(BF16)
            return 0

        lax.fori_loop(0, 8, one, 0, unroll=4)

    @pl.when(guest == 0)
    def _():
        wait_bytes(xf.at[2], c_recv.at[2])
        wait_bytes(xf.at[3], c_recv.at[3])

    @pl.when(guest == 1)
    def _():
        wait_bytes(xf.at[0], c_recv.at[0])
        wait_bytes(xf.at[1], c_recv.at[1])

    for k in range(4):
        transpose(k)

    @pl.when(guest == 0)
    def _():
        wait_bytes(rbuf.at[pl.ds(0, 31 * 16)], r_recv)

    @pl.when(guest == 1)
    def _():
        wait_bytes(rbuf.at[pl.ds(0, 32 * 16)], r_recv)

    mine = pl.ds(pl.multiple_of(512 * guest, 512), 512)
    remote(rbuf.at[mine], rbuf.at[mine], w_send, w_recv, (sib, y)).start()
    wait_bytes(rbuf.at[pl.ds(pl.multiple_of(512 * (1 - guest), 512), 512)], w_recv)

    lane = lax.broadcasted_iota(I32, (8, 128), 1)
    rowi = lax.broadcasted_iota(I32, (8, 128), 0)
    pickrow = jnp.where(lane == rowi, 1.0, 0.0).astype(BF16)
    where = dot_nt(pickrow, rbuf[:, KW:KA]).astype(I32)
    blk = where[0:1]
    row = (blk >> 2) - 32 * core
    key = jnp.where((row >= 0) & (row < 32), where[1:2] * 128 + (blk & 3) * 32 + row, -1)

    def collect(o):
        rows = lax.broadcasted_iota(I32, (128, 1024), 0) + o * 128
        pick = jnp.where(rows == key, 1.0, 0.0).astype(BF16)
        mbuf[o] = dot(pick, rbuf[...]).astype(BF16)

    for o in range(6):
        collect(o)

    def assemble(v):
        for c in range(2):
            for w in range(2):
                acc = None
                for d in range(3):
                    if not 0 <= v - d <= 5:
                        continue
                    start = c * 576 + 96 * (w + 2 * d)
                    base = start // 128 * 128
                    ri = (start - base) // 32
                    term = dot(
                        mbuf[v - d, :, base : base + 256],
                        ebuf[ri * 6 + v - d],
                    )
                    acc = term if acc is None else acc + term
                acc = acc.astype(BF16)
                for a4 in range(4):
                    ks[c * 64 + 8 * v + 4 * w + a4] = jnp.concatenate(
                        [acc[j * 32 : j * 32 + 32, a4 * 64 : a4 * 64 + 64] for j in range(4)], axis=1
                    )

    for v in range(8):
        assemble(v)

    r0 = lax.broadcasted_iota(I32, (256, 256), 0)
    r1 = lax.broadcasted_iota(I32, (256, 256), 1)
    swap = jnp.where((r0 >> 4 == (r1 & 15)) & ((r0 & 15) == r1 >> 4), 1.0, 0.0).astype(BF16)

    def turn(n, _):
        arow = pl.ds(pl.multiple_of(n // 2 * 16, 16), 16)
        irow = pl.ds(pl.multiple_of(lax.rem(n, 2) * 16, 16), 16)
        part = ks[arow, irow, :].reshape(256, 256)
        lb[irow, arow, :] = dot(swap, part).astype(BF16).reshape(16, 16, 256)
        return 0

    lax.fori_loop(0, 16, turn, 0, unroll=2)

    def multiply(kinds):
        def one(i, _):
            ids = [pats[j, 32 * core + i] for j in range(4)]
            right_side = jnp.concatenate(
                [jnp.concatenate([xf[k, n] for n in ids], axis=0) for k in kinds], axis=1
            )
            out = dot(lb[i], right_side).astype(BF16)
            at = pl.ds(pl.multiple_of(i * 64, 64), 64)
            for n, k in enumerate(kinds):
                pb[k, at, 0:128] = out[0:64, n * 128 : n * 128 + 128]
                pb[k, at, 128:256] = out[64:128, n * 128 : n * 128 + 128]
            return 0

        lax.fori_loop(0, 32, one, 0, unroll=4)

    def gram(q):
        g = dot(xt[...], pb[q])
        for a in range(4):
            for b in range(8):
                at = pl.ds(pl.multiple_of(order[a] * 64 + (b // 2) * 16, 16), 16)
                gst[b % 2, q, at, :] = g[a * 128 + b * 16 : a * 128 + b * 16 + 16]
        remote(gst.at[1 - core, q], d0.at[q], d_send.at[q], d_recv.at[q], (sib, y)).start()

    def pair_sum(q):
        wait_bytes(d0.at[q], d_recv.at[q])
        hs[q - 1] = (gst[core, q] + d0[q]).astype(BF16)
        remote(hs.at[q - 1], hr.at[y], h_send.at[q - 1], h_recv.at[y], (me, order[q])).start()

    multiply((2, 3))
    gram(3)
    gram(2)
    pair_sum(3)
    multiply((0, 1))
    pair_sum(2)
    gram(1)
    gram(0)
    pair_sum(1)
    wait_bytes(d0.at[0], d_recv.at[0])
    total = gst[core, 0] + d0[0]
    for yy in (y2, y3, y1):
        wait_bytes(hr.at[yy], h_recv.at[yy])
        total = total + hr[yy].astype(F32)
    tot[...] = total.reshape(16, 16, 256)

    for dz, dx in FAR:
        q = chip_at(dz, dx)
        remote(tot.at[q], tr.at[p], t_send, t_recv, (q * 2 + core, y)).start()
    tr[p] = tot[p]
    wait_bytes(tr.at[pl.ds(0, 15)], t_recv)
    out[...] = jnp.sum(tr[...], axis=0)

    wait_bytes(send_m.at[pl.ds(0, 62)], sm_send)
    wait_bytes(rbuf.at[mine], w_send)
    wait_bytes(xf.at[0], b_send)
    wait_bytes(xf.at[pl.ds(0, 2)], c_send)

    @pl.when(guest == 0)
    def _():
        wait_bytes(send_r.at[pl.ds(0, 31 * 16)], r_send)

    @pl.when(guest == 1)
    def _():
        wait_bytes(send_r, r_send)
        wait_bytes(xf.at[0], e_send)

    for q in range(4):
        wait_bytes(d0.at[q], d_send.at[q])
    for q in range(3):
        wait_bytes(hs.at[q], h_send.at[q])
    wait_bytes(tot.at[pl.ds(0, 15)], t_send)


def body(elem_records, elem_owner, elem_block, elem_offset, modes, mode_readers, pattern):
    dma = pltpu.SemaphoreType.DMA
    vm = pl.BlockSpec(memory_space=pltpu.VMEM)
    out = pl.pallas_call(
        kernel,
        out_shape=jax.ShapeDtypeStruct((16, 256), F32),
        in_specs=[vm] * 7,
        out_specs=vm,
        scratch_shapes=[
            pltpu.VMEM((NQ, BS, COLS), BF16),
            pltpu.VMEM((5, NQ, BS, COLS), BF16),
            pltpu.VMEM((512, KA), BF16),
            pltpu.VMEM((1024, KA), BF16),
            pltpu.VMEM((24, 256, 256), BF16),
            pltpu.VMEM((6, 128, KA), BF16),
            pltpu.VMEM((128, 32, 256), BF16),
            pltpu.VMEM((32, 128, 256), BF16),
            pltpu.VMEM((512, 2048), BF16),
            pltpu.VMEM((4, 2048, 256), BF16),
            pltpu.VMEM((2, 4, 256, 256), F32),
            pltpu.VMEM((4, 256, 256), F32),
            pltpu.VMEM((3, 256, 256), BF16),
            pltpu.VMEM((4, 256, 256), BF16),
            pltpu.VMEM((16, 16, 256), F32),
            pltpu.VMEM((16, 16, 256), F32),
            dma, dma((16,)), dma, dma, dma, dma, dma, dma((16,)), dma, dma((4,)),
            dma, dma((16,)), dma((4,)), dma((4,)), dma((3,)), dma((4,)), dma, dma,
            pltpu.VMEM((8, 128), I32), pltpu.VMEM((8, 128), I32), pltpu.SMEM((8, 128), I32), pltpu.SMEM((8, 128), I32),
            dma, dma, dma, dma,
        ],
        compiler_params=pltpu.CompilerParams(
            collective_id=0, has_side_effects=True, vmem_limit_bytes=60 << 20
        ),
        name="sweep",
    )(
        pattern.T, elem_records, elem_owner.T, elem_block.reshape(1, 256), elem_offset.reshape(1, 256),
        modes, mode_readers.T,
    )
    return out[:, 0:128], out[:, 128:256]


def solution(mesh):
    in_specs = (
        P(("sub", "col"), None),
        P(("sub", "col"), None),
        P(("sub", "col")),
        P(("sub", "col")),
        P("sub", None, "col"),
        P("sub", None),
        P("sub", None),
    )
    out_specs = (P("sub", "col"), P("sub", "col"))
    return jax.shard_map(body, mesh=mesh, in_specs=in_specs, out_specs=out_specs, check_vma=False)
```

```python
import functools

import jax
import jax.numpy as jnp
from jax import lax
from jax.experimental import pallas as pl
from jax.experimental.pallas import tpu as pltpu
from jax.sharding import PartitionSpec as P

MESH = pl.DeviceIdType.MESH
BF16 = jnp.bfloat16
F32 = jnp.float32
I32 = jnp.int32

BS = 64
NQ = 64
NNZ = 4
KW = 1152
KA = 1280
COLS = 128
SLOTS_E = 16


def dot(a, b):
    return jnp.dot(a, b, preferred_element_type=F32)


def dot_nt(a, b):
    return lax.dot_general(a, b, (((1,), (1,)), ((), ())), preferred_element_type=F32)


FAR = (
    (2, 2), (2, 0), (0, 2), (3, 2), (2, 3), (1, 2), (2, 1), (3, 1),
    (1, 3), (3, 3), (1, 1), (3, 0), (0, 3), (1, 0), (0, 1),
)


def kernel(
    pat, rec, owner_row, block_row, offset_row, modes, readers,
    out,
    send_m, xf, send_r, rbuf, ebuf, mbuf, ks, lb, xt, pb, gst, d0, hs, hr, tot, tr,
    sm_send, a_recv, r_send, r_recv, w_send, w_recv, b_send, b_recv, c_send, c_recv,
    e_send, e_recv, d_send, d_recv, h_send, h_recv, t_send, t_recv, tab, patv, pats, mids, p_send, p_recv, p_copy, m_copy, half,
):
    me = lax.axis_index("sub")
    y = lax.axis_index("col")
    core = lax.rem(me, 2)
    p = me // 2
    z = p // 4
    x = lax.rem(p, 4)
    sib = p * 2 + 1 - core
    host = y // 2
    guest = lax.rem(core + host, 2)
    own = 4 * guest
    y1 = y + 1 - 2 * lax.rem(y, 2)
    y3 = 3 - y
    y2 = 3 - y1
    order = (y, y1, y3, y2)

    def chip_at(dz, dx):
        return lax.rem(z + dz, 4) * 4 + lax.rem(x + dx, 4)

    def remote(src, dst, ssem, rsem, dev):
        return pltpu.make_async_remote_copy(
            src_ref=src, dst_ref=dst, send_sem=ssem, recv_sem=rsem, device_id=dev, device_id_type=MESH
        )

    def wait_bytes(ref, sem):
        pltpu.make_async_copy(ref, ref, sem).wait()

    barrier = pltpu.get_barrier_semaphore()

    def hello(dev):
        pl.semaphore_signal(barrier, inc=1, device_id=dev, device_id_type=MESH)

    hello((sib, y))
    for yy in order[1:]:
        for cc in range(2):
            hello((p * 2 + cc, yy))

    def greet(g, _):
        q = chip_at(g // 4, lax.rem(g, 4))
        for cc in range(2):
            hello((q * 2 + cc, y))
        return 0

    lax.fori_loop(1, 16, greet, 0)

    @pl.when(guest == 1)
    def _():
        def greet_far(g, _):
            hello((g, y3))
            return 0

        lax.fori_loop(0, 32, greet_far, 0)

    def iota(shape, axis):
        return lax.broadcasted_iota(I32, shape, axis)

    def eye(n):
        return jnp.where(iota((n, n), 0) == iota((n, n), 1), 1.0, 0.0).astype(BF16)

    named = dot_nt(eye(16), readers[...].astype(F32).astype(BF16))
    subs = iota((16, 32), 1).astype(F32)
    occurs = jnp.where((named[:, 0:1] == subs) | (named[:, 1:2] == subs), 1.0, 0.0)
    lower = jnp.where(iota((16, 16), 0) > iota((16, 16), 1), 1.0, 0.0).astype(BF16)
    ahead = dot(lower, occurs.astype(BF16))
    number = (iota((16, 32), 0) + 1).astype(F32)
    tab[...] = jnp.zeros((8, 128), I32)
    tab[0:4, 0:64] = pat[...]
    for n in range(2):
        picked = jnp.sum(jnp.where((occurs > 0) & (ahead == n), number, 0.0), axis=0, keepdims=True)
        tab[4 + n : 5 + n, 0:32] = picked.astype(I32) - 1
    to_mids = pltpu.make_async_copy(tab, mids, m_copy)
    to_mids.start()

    lines = iota((128, 256), 0)
    facts = jnp.where(
        lines == 0, block_row[...], jnp.where(lines == 1, offset_row[...], jnp.where(lines == 2, owner_row[...], 0))
    ).astype(F32).astype(BF16)
    place = dot_nt(eye(256), facts)
    before = iota((256, 256), 0) < iota((256, 256), 1)
    same = place[:, 2:3] == owner_row[...].astype(F32)
    rank = jnp.sum(jnp.where(same & before, 1, 0), axis=0, keepdims=True)
    pos = owner_row[...] * SLOTS_E + rank
    place = place.astype(BF16)

    def permute(g, _):
        pick = jnp.where(iota((128, 256), 0) + g * 128 == pos, 1.0, 0.0).astype(BF16)
        at = pl.ds(pl.multiple_of(g * 128, 128), 128)
        send_r[at, 0:KW] = dot(pick, rec[...]).astype(BF16)
        send_r[at, KW:KA] = dot(pick, place).astype(BF16)
        return 0

    lax.fori_loop(0, 4, permute, 0)

    to_mids.wait()

    def fill(s, _):
        k = mids[4 + lax.rem(s, 2), s // 2]
        block = modes[jnp.clip(k, 0, modes.shape[0] - 1)]
        send_m[s] = jnp.where(k >= 0, block, jnp.zeros_like(block))
        return 0

    lax.fori_loop(0, NQ, fill, 0, unroll=4)

    pl.semaphore_wait(barrier, 53)

    xf[own, pl.ds(2 * me, 2)] = send_m[pl.ds(2 * me, 2)]

    @pl.when(guest == 0)
    def _():
        away = remote(tab, patv, p_send, p_recv, (sib, y))
        away.start()
        here = pltpu.make_async_copy(tab, pats, p_copy)
        here.start()
        away.wait_send()
        here.wait()

    def other(cc):
        return lax.rem(cc + host, 2)

    def send_mode(dest, lands):
        remote(
            send_m.at[pl.ds(2 * dest, 2)], xf.at[lands, pl.ds(2 * me, 2)], sm_send, a_recv.at[p], (dest, y)
        ).start()

    def rows16(n):
        return pl.ds(pl.multiple_of(n * 16, 16), 16)

    def send_rec(q, cc):
        far = other(cc)
        remote(
            send_r.at[rows16(q * 2 + cc)], rbuf.at[rows16(32 * far + me)], r_send, r_recv,
            (q * 2 + host, y + far * (y3 - y)),
        ).start()

    send_mode(sib, 4 * (1 - guest))
    for dz, dx in FAR:
        q = chip_at(dz, dx)
        for cc in range(2):
            send_mode(q * 2 + cc, 4 * other(cc))

    @pl.when(guest == 0)
    def _():
        rbuf[rows16(me)] = send_r[rows16(me)]

    remote(
        send_r.at[rows16(p * 2 + 1 - host)], rbuf.at[rows16(32 + me)], r_send, r_recv, (p * 2 + host, y3)
    ).start()

    @pl.when(guest == 1)
    def _():
        remote(send_r.at[rows16(sib)], rbuf.at[rows16(me)], r_send, r_recv, (sib, y)).start()

    def first(q, fresh):
        at = pl.ds(4 * q, 4)
        wait_bytes(fresh, a_recv.at[q])
        remote(
            xf.at[own, at], xf.at[1 + guest, at], b_send, b_recv.at[q],
            (me + guest * (sib - me), y1 + guest * (y3 - y1)),
        ).start()

        @pl.when(guest == 0)
        def _():
            remote(xf.at[0, at], xf.at[0, at], c_send, c_recv.at[0], (sib, y)).start()

    def second(q):
        at = pl.ds(4 * q, 4)
        wait_bytes(xf.at[1 + guest, at], b_recv.at[q])

        @pl.when(guest == 1)
        def _():
            remote(xf.at[2, at], xf.at[3, at], e_send, e_recv.at[q], (me, y1)).start()

        remote(xf.at[1 + guest, at], xf.at[1 + guest, at], c_send, c_recv.at[1 + guest], (sib, y)).start()

    def third(q):
        at = pl.ds(4 * q, 4)

        @pl.when(guest == 1)
        def _():
            wait_bytes(xf.at[3, at], e_recv.at[q])
            remote(xf.at[3, at], xf.at[3, at], c_send, c_recv.at[3], (sib, y)).start()

    chips = [p] + [chip_at((4 - dz) % 4, (4 - dx) % 4) for dz, dx in FAR]
    for n, q in enumerate(chips):
        first(q, xf.at[own, pl.ds(2 * sib, 2)] if n == 0 else xf.at[own, pl.ds(4 * q, 4)])
    for cc in (host, 1 - host):
        for dz, dx in FAR:
            send_rec(chip_at(dz, dx), cc)

    def place_matrix(n, _):
        ri = n // 6
        o = lax.rem(n, 6)
        k = lax.broadcasted_iota(I32, (256, 256), 0)
        col = lax.broadcasted_iota(I32, (256, 256), 1)
        bb = (col & 63) - 8 * o
        hit = (k == 32 * ri + (col >> 6) * 24 + bb) & (bb >= 0) & (bb < 24)
        ebuf[n] = jnp.where(hit, 1.0, 0.0).astype(BF16)
        return 0

    lax.fori_loop(0, 24, place_matrix, 0)

    for q in chips:
        second(q)
    for q in chips:
        third(q)

    @pl.when(guest == 1)
    def _():
        wait_bytes(patv, p_recv)
        here = pltpu.make_async_copy(patv, pats, p_copy)
        here.start()
        here.wait()

    @pl.when(guest == 0)
    def _():
        wait_bytes(rbuf.at[pl.ds(0, 31 * 16)], r_recv)

    @pl.when(guest == 1)
    def _():
        wait_bytes(rbuf.at[pl.ds(0, 32 * 16)], r_recv)

    mine = pl.ds(pl.multiple_of(512 * guest, 512), 512)
    remote(rbuf.at[mine], rbuf.at[mine], w_send, w_recv, (sib, y)).start()

    turned = eye(128)

    def transpose(k):
        def one(g, _):
            part = xf[k, pl.ds(32 * core + 4 * g, 4)].reshape(256, COLS)
            xt[k * 128 : k * 128 + 128, pl.ds(pl.multiple_of(g * 256, 256), 256)] = dot_nt(turned, part).astype(BF16)
            return 0

        lax.fori_loop(0, 8, one, 0, unroll=8)

    @pl.when(guest == 0)
    def _():
        wait_bytes(xf.at[2], c_recv.at[2])
        wait_bytes(xf.at[3], c_recv.at[3])

    @pl.when(guest == 1)
    def _():
        wait_bytes(xf.at[0], c_recv.at[0])
        wait_bytes(xf.at[1], c_recv.at[1])

    for k in range(4):
        transpose(k)

    pickrow = jnp.where(iota((8, 128), 0) == iota((8, 128), 1), 1.0, 0.0).astype(BF16)

    def collect(rows, last):
        facts = dot_nt(pickrow, rbuf[rows, KW:KA]).astype(I32)
        blk = facts[0:1]
        row = (blk >> 2) - 32 * core
        key = jnp.where((row >= 0) & (row < 32), facts[1:2] * 128 + (blk & 3) * 32 + row, -1)
        for o in range(6):
            pick = jnp.where(iota((128, 512), 0) + o * 128 == key, 1.0, 0.0).astype(BF16)
            part = dot(pick, rbuf[rows, :])
            if last:
                mbuf[o] = (half[o] + part).astype(BF16)
            else:
                half[o] = part

    collect(mine, False)
    wait_bytes(rbuf.at[pl.ds(pl.multiple_of(512 * (1 - guest), 512), 512)], w_recv)
    collect(pl.ds(pl.multiple_of(512 * (1 - guest), 512), 512), True)

    def assemble(v):
        for c in range(2):
            for w in range(2):
                acc = None
                for d in range(3):
                    if not 0 <= v - d <= 5:
                        continue
                    start = c * 576 + 96 * (w + 2 * d)
                    base = start // 128 * 128
                    ri = (start - base) // 32
                    term = dot(
                        mbuf[v - d, :, base : base + 256],
                        ebuf[ri * 6 + v - d],
                    )
                    acc = term if acc is None else acc + term
                acc = acc.astype(BF16)
                for a4 in range(4):
                    ks[c * 64 + 8 * v + 4 * w + a4] = jnp.concatenate(
                        [acc[j * 32 : j * 32 + 32, a4 * 64 : a4 * 64 + 64] for j in range(4)], axis=1
                    )

    for v in range(8):
        assemble(v)

    r0 = lax.broadcasted_iota(I32, (256, 256), 0)
    r1 = lax.broadcasted_iota(I32, (256, 256), 1)
    swap = jnp.where((r0 >> 4 == (r1 & 15)) & ((r0 & 15) == r1 >> 4), 1.0, 0.0).astype(BF16)

    def turn(n, _):
        arow = pl.ds(pl.multiple_of(n // 2 * 16, 16), 16)
        irow = pl.ds(pl.multiple_of(lax.rem(n, 2) * 16, 16), 16)
        part = ks[arow, irow, :].reshape(256, 256)
        lb[irow, arow, :] = dot(swap, part).astype(BF16).reshape(16, 16, 256)
        return 0

    lax.fori_loop(0, 16, turn, 0, unroll=8)

    def multiply(kinds):
        def one(i, _):
            ids = [pats[j, 32 * core + i] for j in range(4)]
            right_side = jnp.concatenate(
                [jnp.concatenate([xf[k, n] for n in ids], axis=0) for k in kinds], axis=1
            )
            out = dot(lb[i], right_side).astype(BF16)
            at = pl.ds(pl.multiple_of(i * 64, 64), 64)
            for n, k in enumerate(kinds):
                pb[k, at, 0:128] = out[0:64, n * 128 : n * 128 + 128]
                pb[k, at, 128:256] = out[64:128, n * 128 : n * 128 + 128]
            return 0

        lax.fori_loop(0, 32, one, 0, unroll=8)

    def gram(q):
        g = dot(xt[...], pb[q])
        for a in range(4):
            for b in range(8):
                at = pl.ds(pl.multiple_of(order[a] * 64 + (b // 2) * 16, 16), 16)
                gst[b % 2, q, at, :] = g[a * 128 + b * 16 : a * 128 + b * 16 + 16]
        remote(gst.at[1 - core, q], d0.at[q], d_send.at[q], d_recv.at[q], (sib, y)).start()

    def pair_sum(q):
        wait_bytes(d0.at[q], d_recv.at[q])
        hs[q - 1] = (gst[core, q] + d0[q]).astype(BF16)
        remote(hs.at[q - 1], hr.at[y], h_send.at[q - 1], h_recv.at[y], (me, order[q])).start()

    multiply((2, 3))
    gram(3)
    gram(2)
    pair_sum(3)
    multiply((0, 1))
    pair_sum(2)
    gram(1)
    pair_sum(1)
    gram(0)
    wait_bytes(d0.at[0], d_recv.at[0])
    total = gst[core, 0] + d0[0]
    for yy in (y2, y3, y1):
        wait_bytes(hr.at[yy], h_recv.at[yy])
        total = total + hr[yy].astype(F32)
    tot[...] = total.reshape(16, 16, 256)

    for dz, dx in FAR:
        q = chip_at(dz, dx)
        remote(tot.at[q], tr.at[p], t_send, t_recv, (q * 2 + core, y)).start()
    tr[p] = tot[p]
    wait_bytes(tr.at[pl.ds(0, 15)], t_recv)
    out[...] = jnp.sum(tr[...], axis=0)

    wait_bytes(send_m.at[pl.ds(0, 62)], sm_send)
    wait_bytes(rbuf.at[mine], w_send)
    wait_bytes(xf.at[0], b_send)
    wait_bytes(xf.at[pl.ds(0, 2)], c_send)

    @pl.when(guest == 0)
    def _():
        wait_bytes(send_r.at[pl.ds(0, 31 * 16)], r_send)

    @pl.when(guest == 1)
    def _():
        wait_bytes(send_r, r_send)
        wait_bytes(xf.at[0], e_send)

    for q in range(4):
        wait_bytes(d0.at[q], d_send.at[q])
    for q in range(3):
        wait_bytes(hs.at[q], h_send.at[q])
    wait_bytes(tot.at[pl.ds(0, 15)], t_send)


def body(elem_records, elem_owner, elem_block, elem_offset, modes, mode_readers, pattern):
    dma = pltpu.SemaphoreType.DMA
    vm = pl.BlockSpec(memory_space=pltpu.VMEM)
    out = pl.pallas_call(
        kernel,
        out_shape=jax.ShapeDtypeStruct((16, 256), F32),
        in_specs=[vm] * 7,
        out_specs=vm,
        scratch_shapes=[
            pltpu.VMEM((NQ, BS, COLS), BF16),
            pltpu.VMEM((5, NQ, BS, COLS), BF16),
            pltpu.VMEM((512, KA), BF16),
            pltpu.VMEM((1024, KA), BF16),
            pltpu.VMEM((24, 256, 256), BF16),
            pltpu.VMEM((6, 128, KA), BF16),
            pltpu.VMEM((128, 32, 256), BF16),
            pltpu.VMEM((32, 128, 256), BF16),
            pltpu.VMEM((512, 2048), BF16),
            pltpu.VMEM((4, 2048, 256), BF16),
            pltpu.VMEM((2, 4, 256, 256), F32),
            pltpu.VMEM((4, 256, 256), F32),
            pltpu.VMEM((3, 256, 256), BF16),
            pltpu.VMEM((4, 256, 256), BF16),
            pltpu.VMEM((16, 16, 256), F32),
            pltpu.VMEM((16, 16, 256), F32),
            dma, dma((16,)), dma, dma, dma, dma, dma, dma((16,)), dma, dma((4,)),
            dma, dma((16,)), dma((4,)), dma((4,)), dma((3,)), dma((4,)), dma, dma,
            pltpu.VMEM((8, 128), I32), pltpu.VMEM((8, 128), I32), pltpu.SMEM((8, 128), I32), pltpu.SMEM((8, 128), I32),
            dma, dma, dma, dma, pltpu.VMEM((6, 128, KA), F32),
        ],
        compiler_params=pltpu.CompilerParams(
            collective_id=0, has_side_effects=True, vmem_limit_bytes=60 << 20
        ),
        name="sweep",
    )(
        pattern.T, elem_records, elem_owner.T, elem_block.reshape(1, 256), elem_offset.reshape(1, 256),
        modes, mode_readers.T,
    )
    return out[:, 0:128], out[:, 128:256]


def solution(mesh):
    in_specs = (
        P(("sub", "col"), None),
        P(("sub", "col"), None),
        P(("sub", "col")),
        P(("sub", "col")),
        P("sub", None, "col"),
        P("sub", None),
        P("sub", None),
    )
    out_specs = (P("sub", "col"), P("sub", "col"))
    return jax.shard_map(body, mesh=mesh, in_specs=in_specs, out_specs=out_specs, check_vma=False)
```

```python
import functools

import jax
import jax.numpy as jnp
from jax import lax
from jax.experimental import pallas as pl
from jax.experimental.pallas import tpu as pltpu
from jax.sharding import PartitionSpec as P

MESH = pl.DeviceIdType.MESH
BF16 = jnp.bfloat16
F32 = jnp.float32
I32 = jnp.int32

BS = 64
NQ = 64
NNZ = 4
KW = 1152
KA = 1280
COLS = 128
SLOTS_E = 16


def dot(a, b):
    return jnp.dot(a, b, preferred_element_type=F32)


def dot_nt(a, b):
    return lax.dot_general(a, b, (((1,), (1,)), ((), ())), preferred_element_type=F32)


FAR = (
    (2, 2), (2, 0), (0, 2), (3, 2), (2, 3), (1, 2), (2, 1), (3, 1),
    (1, 3), (3, 3), (1, 1), (3, 0), (0, 3), (1, 0), (0, 1),
)


def kernel(
    pat, rec, owner_row, block_row, offset_row, modes, readers,
    out,
    send_m, xf, send_r, rbuf, ebuf, mbuf, ks, lb, xt, pb, gst, d0, hs, hr, tot, tr,
    sm_send, a_recv, r_send, r_recv, w_send, w_recv, b_send, b_recv, c_send, c_recv,
    e_send, e_recv, d_send, d_recv, h_send, h_recv, t_send, t_recv, tab, patv, pats, mids, p_send, p_recv, p_copy, m_copy, half,
):
    me = lax.axis_index("sub")
    y = lax.axis_index("col")
    core = lax.rem(me, 2)
    p = me // 2
    z = p // 4
    x = lax.rem(p, 4)
    sib = p * 2 + 1 - core
    host = y // 2
    guest = lax.rem(core + host, 2)
    own = 4 * guest
    y1 = y + 1 - 2 * lax.rem(y, 2)
    y3 = 3 - y
    y2 = 3 - y1
    order = (y, y1, y3, y2)

    def chip_at(dz, dx):
        return lax.rem(z + dz, 4) * 4 + lax.rem(x + dx, 4)

    def remote(src, dst, ssem, rsem, dev):
        return pltpu.make_async_remote_copy(
            src_ref=src, dst_ref=dst, send_sem=ssem, recv_sem=rsem, device_id=dev, device_id_type=MESH
        )

    def wait_bytes(ref, sem):
        pltpu.make_async_copy(ref, ref, sem).wait()

    barrier = pltpu.get_barrier_semaphore()

    def hello(dev):
        pl.semaphore_signal(barrier, inc=1, device_id=dev, device_id_type=MESH)

    hello((sib, y))
    for yy in order[1:]:
        for cc in range(2):
            hello((p * 2 + cc, yy))

    def greet(g, _):
        q = chip_at(g // 4, lax.rem(g, 4))
        for cc in range(2):
            hello((q * 2 + cc, y))
        return 0

    lax.fori_loop(1, 16, greet, 0)

    @pl.when(guest == 1)
    def _():
        def greet_far(g, _):
            hello((g, y3))
            return 0

        lax.fori_loop(0, 32, greet_far, 0)

    def iota(shape, axis):
        return lax.broadcasted_iota(I32, shape, axis)

    def eye(n):
        return jnp.where(iota((n, n), 0) == iota((n, n), 1), 1.0, 0.0).astype(BF16)

    named = dot_nt(eye(16), readers[...].astype(F32).astype(BF16))
    subs = iota((16, 32), 1).astype(F32)
    occurs = jnp.where((named[:, 0:1] == subs) | (named[:, 1:2] == subs), 1.0, 0.0)
    lower = jnp.where(iota((16, 16), 0) > iota((16, 16), 1), 1.0, 0.0).astype(BF16)
    ahead = dot(lower, occurs.astype(BF16))
    number = (iota((16, 32), 0) + 1).astype(F32)
    tab[...] = jnp.zeros((8, 128), I32)
    tab[0:4, 0:64] = pat[...]
    for n in range(2):
        picked = jnp.sum(jnp.where((occurs > 0) & (ahead == n), number, 0.0), axis=0, keepdims=True)
        tab[4 + n : 5 + n, 0:32] = picked.astype(I32) - 1
    to_mids = pltpu.make_async_copy(tab, mids, m_copy)
    to_mids.start()

    lines = iota((128, 256), 0)
    facts = jnp.where(
        lines == 0, block_row[...], jnp.where(lines == 1, offset_row[...], jnp.where(lines == 2, owner_row[...], 0))
    ).astype(F32).astype(BF16)
    place = dot_nt(eye(256), facts)
    before = iota((256, 256), 0) < iota((256, 256), 1)
    same = place[:, 2:3] == owner_row[...].astype(F32)
    rank = jnp.sum(jnp.where(same & before, 1, 0), axis=0, keepdims=True)
    pos = owner_row[...] * SLOTS_E + rank
    place = place.astype(BF16)

    def permute(g, _):
        pick = jnp.where(iota((128, 256), 0) + g * 128 == pos, 1.0, 0.0).astype(BF16)
        at = pl.ds(pl.multiple_of(g * 128, 128), 128)
        send_r[at, 0:KW] = dot(pick, rec[...]).astype(BF16)
        send_r[at, KW:KA] = dot(pick, place).astype(BF16)
        return 0

    lax.fori_loop(0, 4, permute, 0)

    to_mids.wait()

    def fill(s, _):
        k = mids[4 + lax.rem(s, 2), s // 2]
        block = modes[jnp.clip(k, 0, modes.shape[0] - 1)]
        send_m[s] = jnp.where(k >= 0, block, jnp.zeros_like(block))
        return 0

    lax.fori_loop(0, NQ, fill, 0, unroll=4)

    pl.semaphore_wait(barrier, 53)

    xf[own, pl.ds(2 * me, 2)] = send_m[pl.ds(2 * me, 2)]

    @pl.when(guest == 0)
    def _():
        away = remote(tab, patv, p_send, p_recv, (sib, y))
        away.start()
        here = pltpu.make_async_copy(tab, pats, p_copy)
        here.start()
        away.wait_send()
        here.wait()

    def other(cc):
        return lax.rem(cc + host, 2)

    def send_mode(dest, lands):
        remote(
            send_m.at[pl.ds(2 * dest, 2)], xf.at[lands, pl.ds(2 * me, 2)], sm_send, a_recv.at[p], (dest, y)
        ).start()

    def rows16(n):
        return pl.ds(pl.multiple_of(n * 16, 16), 16)

    def send_rec(q, cc):
        far = other(cc)
        remote(
            send_r.at[rows16(q * 2 + cc)], rbuf.at[rows16(32 * far + me)], r_send, r_recv,
            (q * 2 + host, y + far * (y3 - y)),
        ).start()

    send_mode(sib, 4 * (1 - guest))
    for dz, dx in FAR:
        q = chip_at(dz, dx)
        for cc in range(2):
            send_mode(q * 2 + cc, 4 * other(cc))

    @pl.when(guest == 0)
    def _():
        rbuf[rows16(me)] = send_r[rows16(me)]

    remote(
        send_r.at[rows16(p * 2 + 1 - host)], rbuf.at[rows16(32 + me)], r_send, r_recv, (p * 2 + host, y3)
    ).start()

    @pl.when(guest == 1)
    def _():
        remote(send_r.at[rows16(sib)], rbuf.at[rows16(me)], r_send, r_recv, (sib, y)).start()

    def first(q, fresh):
        at = pl.ds(4 * q, 4)
        wait_bytes(fresh, a_recv.at[q])
        remote(
            xf.at[own, at], xf.at[1 + guest, at], b_send, b_recv.at[q],
            (me + guest * (sib - me), y1 + guest * (y3 - y1)),
        ).start()

        @pl.when(guest == 0)
        def _():
            remote(xf.at[0, at], xf.at[0, at], c_send, c_recv.at[0], (sib, y)).start()

    def second(q):
        at = pl.ds(4 * q, 4)
        wait_bytes(xf.at[1 + guest, at], b_recv.at[q])

        @pl.when(guest == 1)
        def _():
            remote(xf.at[2, at], xf.at[3, at], e_send, e_recv.at[q], (me, y1)).start()

        remote(xf.at[1 + guest, at], xf.at[1 + guest, at], c_send, c_recv.at[1 + guest], (sib, y)).start()

    def third(q):
        at = pl.ds(4 * q, 4)

        @pl.when(guest == 1)
        def _():
            wait_bytes(xf.at[3, at], e_recv.at[q])
            remote(xf.at[3, at], xf.at[3, at], c_send, c_recv.at[3], (sib, y)).start()

    chips = [p] + [chip_at((4 - dz) % 4, (4 - dx) % 4) for dz, dx in FAR]
    for n, q in enumerate(chips):
        first(q, xf.at[own, pl.ds(2 * sib, 2)] if n == 0 else xf.at[own, pl.ds(4 * q, 4)])
    for cc in (host, 1 - host):
        for dz, dx in FAR:
            send_rec(chip_at(dz, dx), cc)

    def place_matrix(n, _):
        ri = n // 6
        o = lax.rem(n, 6)
        k = lax.broadcasted_iota(I32, (256, 256), 0)
        col = lax.broadcasted_iota(I32, (256, 256), 1)
        bb = (col & 63) - 8 * o
        hit = (k == 32 * ri + (col >> 6) * 24 + bb) & (bb >= 0) & (bb < 24)
        ebuf[n] = jnp.where(hit, 1.0, 0.0).astype(BF16)
        return 0

    lax.fori_loop(0, 24, place_matrix, 0)

    for q in chips:
        second(q)
    for q in chips:
        third(q)

    @pl.when(guest == 1)
    def _():
        wait_bytes(patv, p_recv)
        here = pltpu.make_async_copy(patv, pats, p_copy)
        here.start()
        here.wait()

    @pl.when(guest == 0)
    def _():
        wait_bytes(rbuf.at[pl.ds(0, 31 * 16)], r_recv)

    @pl.when(guest == 1)
    def _():
        wait_bytes(rbuf.at[pl.ds(0, 32 * 16)], r_recv)

    mine = pl.ds(pl.multiple_of(512 * guest, 512), 512)
    remote(rbuf.at[mine], rbuf.at[mine], w_send, w_recv, (sib, y)).start()

    turned = eye(128)

    def transpose(k):
        def one(g, _):
            part = xf[k, pl.ds(32 * core + 4 * g, 4)].reshape(256, COLS)
            xt[pl.ds(pl.multiple_of(k * 128, 128), 128), pl.ds(pl.multiple_of(g * 256, 256), 256)] = dot_nt(turned, part).astype(BF16)
            return 0

        lax.fori_loop(0, 8, one, 0, unroll=8)

    transpose(2 * guest)
    transpose(2 * guest + 1)

    @pl.when(guest == 0)
    def _():
        wait_bytes(xf.at[2], c_recv.at[2])
        wait_bytes(xf.at[3], c_recv.at[3])

    @pl.when(guest == 1)
    def _():
        wait_bytes(xf.at[0], c_recv.at[0])
        wait_bytes(xf.at[1], c_recv.at[1])

    transpose(2 - 2 * guest)
    transpose(3 - 2 * guest)

    pickrow = jnp.where(iota((8, 128), 0) == iota((8, 128), 1), 1.0, 0.0).astype(BF16)

    def collect(rows, last):
        facts = dot_nt(pickrow, rbuf[rows, KW:KA]).astype(I32)
        blk = facts[0:1]
        row = (blk >> 2) - 32 * core
        key = jnp.where((row >= 0) & (row < 32), facts[1:2] * 128 + (blk & 3) * 32 + row, -1)
        for o in range(6):
            pick = jnp.where(iota((128, 512), 0) + o * 128 == key, 1.0, 0.0).astype(BF16)
            part = dot(pick, rbuf[rows, :])
            if last:
                mbuf[o] = (half[o] + part).astype(BF16)
            else:
                half[o] = part

    collect(mine, False)
    wait_bytes(rbuf.at[pl.ds(pl.multiple_of(512 * (1 - guest), 512), 512)], w_recv)
    collect(pl.ds(pl.multiple_of(512 * (1 - guest), 512), 512), True)

    def assemble(v):
        for c in range(2):
            for w in range(2):
                acc = None
                for d in range(3):
                    if not 0 <= v - d <= 5:
                        continue
                    start = c * 576 + 96 * (w + 2 * d)
                    base = start // 128 * 128
                    ri = (start - base) // 32
                    term = dot(
                        mbuf[v - d, :, base : base + 256],
                        ebuf[ri * 6 + v - d],
                    )
                    acc = term if acc is None else acc + term
                acc = acc.astype(BF16)
                for a4 in range(4):
                    ks[c * 64 + 8 * v + 4 * w + a4] = jnp.concatenate(
                        [acc[j * 32 : j * 32 + 32, a4 * 64 : a4 * 64 + 64] for j in range(4)], axis=1
                    )

    for v in range(8):
        assemble(v)

    r0 = lax.broadcasted_iota(I32, (256, 256), 0)
    r1 = lax.broadcasted_iota(I32, (256, 256), 1)
    swap = jnp.where((r0 >> 4 == (r1 & 15)) & ((r0 & 15) == r1 >> 4), 1.0, 0.0).astype(BF16)

    def turn(n, _):
        arow = pl.ds(pl.multiple_of(n // 2 * 16, 16), 16)
        irow = pl.ds(pl.multiple_of(lax.rem(n, 2) * 16, 16), 16)
        part = ks[arow, irow, :].reshape(256, 256)
        lb[irow, arow, :] = dot(swap, part).astype(BF16).reshape(16, 16, 256)
        return 0

    lax.fori_loop(0, 16, turn, 0, unroll=8)

    def multiply(kinds):
        def one(i, _):
            ids = [pats[j, 32 * core + i] for j in range(4)]
            right_side = jnp.concatenate(
                [jnp.concatenate([xf[k, n] for n in ids], axis=0) for k in kinds], axis=1
            )
            out = dot(lb[i], right_side).astype(BF16)
            at = pl.ds(pl.multiple_of(i * 64, 64), 64)
            for n, k in enumerate(kinds):
                pb[k, at, 0:128] = out[0:64, n * 128 : n * 128 + 128]
                pb[k, at, 128:256] = out[64:128, n * 128 : n * 128 + 128]
            return 0

        lax.fori_loop(0, 32, one, 0, unroll=16)

    def gram(q):
        g = dot(xt[...], pb[q])
        for a in range(4):
            for b in range(8):
                at = pl.ds(pl.multiple_of(order[a] * 64 + (b // 2) * 16, 16), 16)
                gst[b % 2, q, at, :] = g[a * 128 + b * 16 : a * 128 + b * 16 + 16]
        remote(gst.at[1 - core, q], d0.at[q], d_send.at[q], d_recv.at[q], (sib, y)).start()

    def pair_sum(q):
        wait_bytes(d0.at[q], d_recv.at[q])
        hs[q - 1] = (gst[core, q] + d0[q]).astype(BF16)
        remote(hs.at[q - 1], hr.at[y], h_send.at[q - 1], h_recv.at[y], (me, order[q])).start()

    multiply((2, 3))
    gram(3)
    gram(2)
    pair_sum(3)
    multiply((0, 1))
    pair_sum(2)
    gram(1)
    pair_sum(1)
    gram(0)
    wait_bytes(d0.at[0], d_recv.at[0])
    total = gst[core, 0] + d0[0]
    for yy in (y2, y3, y1):
        wait_bytes(hr.at[yy], h_recv.at[yy])
        total = total + hr[yy].astype(F32)
    tot[...] = total.reshape(16, 16, 256)

    for dz, dx in FAR:
        q = chip_at(dz, dx)
        remote(tot.at[q], tr.at[p], t_send, t_recv, (q * 2 + core, y)).start()
    tr[p] = tot[p]
    wait_bytes(tr.at[pl.ds(0, 15)], t_recv)
    out[...] = jnp.sum(tr[...], axis=0)

    wait_bytes(send_m.at[pl.ds(0, 62)], sm_send)
    wait_bytes(rbuf.at[mine], w_send)
    wait_bytes(xf.at[0], b_send)
    wait_bytes(xf.at[pl.ds(0, 2)], c_send)

    @pl.when(guest == 0)
    def _():
        wait_bytes(send_r.at[pl.ds(0, 31 * 16)], r_send)

    @pl.when(guest == 1)
    def _():
        wait_bytes(send_r, r_send)
        wait_bytes(xf.at[0], e_send)

    for q in range(4):
        wait_bytes(d0.at[q], d_send.at[q])
    for q in range(3):
        wait_bytes(hs.at[q], h_send.at[q])
    wait_bytes(tot.at[pl.ds(0, 15)], t_send)


def body(elem_records, elem_owner, elem_block, elem_offset, modes, mode_readers, pattern):
    dma = pltpu.SemaphoreType.DMA
    vm = pl.BlockSpec(memory_space=pltpu.VMEM)
    out = pl.pallas_call(
        kernel,
        out_shape=jax.ShapeDtypeStruct((16, 256), F32),
        in_specs=[vm] * 7,
        out_specs=vm,
        scratch_shapes=[
            pltpu.VMEM((NQ, BS, COLS), BF16),
            pltpu.VMEM((5, NQ, BS, COLS), BF16),
            pltpu.VMEM((512, KA), BF16),
            pltpu.VMEM((1024, KA), BF16),
            pltpu.VMEM((24, 256, 256), BF16),
            pltpu.VMEM((6, 128, KA), BF16),
            pltpu.VMEM((128, 32, 256), BF16),
            pltpu.VMEM((32, 128, 256), BF16),
            pltpu.VMEM((512, 2048), BF16),
            pltpu.VMEM((4, 2048, 256), BF16),
            pltpu.VMEM((2, 4, 256, 256), F32),
            pltpu.VMEM((4, 256, 256), F32),
            pltpu.VMEM((3, 256, 256), BF16),
            pltpu.VMEM((4, 256, 256), BF16),
            pltpu.VMEM((16, 16, 256), F32),
            pltpu.VMEM((16, 16, 256), F32),
            dma, dma((16,)), dma, dma, dma, dma, dma, dma((16,)), dma, dma((4,)),
            dma, dma((16,)), dma((4,)), dma((4,)), dma((3,)), dma((4,)), dma, dma,
            pltpu.VMEM((8, 128), I32), pltpu.VMEM((8, 128), I32), pltpu.SMEM((8, 128), I32), pltpu.SMEM((8, 128), I32),
            dma, dma, dma, dma, pltpu.VMEM((6, 128, KA), F32),
        ],
        compiler_params=pltpu.CompilerParams(
            collective_id=0, has_side_effects=True, vmem_limit_bytes=60 << 20
        ),
        name="sweep",
    )(
        pattern.T, elem_records, elem_owner.T, elem_block.reshape(1, 256), elem_offset.reshape(1, 256),
        modes, mode_readers.T,
    )
    return out[:, 0:128], out[:, 128:256]


def solution(mesh):
    in_specs = (
        P(("sub", "col"), None),
        P(("sub", "col"), None),
        P(("sub", "col")),
        P(("sub", "col")),
        P("sub", None, "col"),
        P("sub", None),
        P("sub", None),
    )
    out_specs = (P("sub", "col"), P("sub", "col"))
    return jax.shard_map(body, mesh=mesh, in_specs=in_specs, out_specs=out_specs, check_vma=False)
```

```python
import functools

import jax
import jax.numpy as jnp
from jax import lax
from jax.experimental import pallas as pl
from jax.experimental.pallas import tpu as pltpu
from jax.sharding import PartitionSpec as P

MESH = pl.DeviceIdType.MESH
BF16 = jnp.bfloat16
F32 = jnp.float32
I32 = jnp.int32

BS = 64
NQ = 64
NNZ = 4
KW = 1152
KA = 1280
COLS = 128
SLOTS_E = 16


def dot(a, b):
    return jnp.dot(a, b, preferred_element_type=F32)


def dot_nt(a, b):
    return lax.dot_general(a, b, (((1,), (1,)), ((), ())), preferred_element_type=F32)


FAR = (
    (2, 2), (2, 0), (0, 2), (3, 2), (2, 3), (1, 2), (2, 1), (3, 1),
    (1, 3), (3, 3), (1, 1), (3, 0), (0, 3), (1, 0), (0, 1),
)


def kernel(
    pat, rec, owner_row, block_row, offset_row, modes, readers,
    out,
    send_m, xf, send_r, rbuf, ebuf, mbuf, ks, lb, xt, pb, gst, d0, hs, hr, tot, tr,
    sm_send, a_recv, r_send, r_recv, w_send, w_recv, b_send, b_recv, c_send, c_recv,
    e_send, e_recv, d_send, d_recv, h_send, h_recv, t_send, t_recv, tab, patv, pats, mids, p_send, p_recv, p_copy, m_copy, half,
):
    me = lax.axis_index("sub")
    y = lax.axis_index("col")
    core = lax.rem(me, 2)
    p = me // 2
    z = p // 4
    x = lax.rem(p, 4)
    sib = p * 2 + 1 - core
    host = y // 2
    guest = lax.rem(core + host, 2)
    own = 4 * guest
    y1 = y + 1 - 2 * lax.rem(y, 2)
    y3 = 3 - y
    y2 = 3 - y1
    order = (y, y1, y3, y2)

    def chip_at(dz, dx):
        return lax.rem(z + dz, 4) * 4 + lax.rem(x + dx, 4)

    def remote(src, dst, ssem, rsem, dev):
        return pltpu.make_async_remote_copy(
            src_ref=src, dst_ref=dst, send_sem=ssem, recv_sem=rsem, device_id=dev, device_id_type=MESH
        )

    def wait_bytes(ref, sem):
        pltpu.make_async_copy(ref, ref, sem).wait()

    barrier = pltpu.get_barrier_semaphore()

    def hello(dev):
        pl.semaphore_signal(barrier, inc=1, device_id=dev, device_id_type=MESH)

    hello((sib, y))
    for yy in order[1:]:
        for cc in range(2):
            hello((p * 2 + cc, yy))

    def greet(g, _):
        q = chip_at(g // 4, lax.rem(g, 4))
        for cc in range(2):
            hello((q * 2 + cc, y))
        return 0

    lax.fori_loop(1, 16, greet, 0)

    @pl.when(guest == 1)
    def _():
        def greet_far(g, _):
            hello((g, y3))
            return 0

        lax.fori_loop(0, 32, greet_far, 0)

    def iota(shape, axis):
        return lax.broadcasted_iota(I32, shape, axis)

    def eye(n):
        return jnp.where(iota((n, n), 0) == iota((n, n), 1), 1.0, 0.0).astype(BF16)

    named = dot_nt(eye(16), readers[...].astype(F32).astype(BF16))
    subs = iota((16, 32), 1).astype(F32)
    occurs = jnp.where((named[:, 0:1] == subs) | (named[:, 1:2] == subs), 1.0, 0.0)
    lower = jnp.where(iota((16, 16), 0) > iota((16, 16), 1), 1.0, 0.0).astype(BF16)
    ahead = dot(lower, occurs.astype(BF16))
    number = (iota((16, 32), 0) + 1).astype(F32)
    tab[...] = jnp.zeros((8, 128), I32)
    tab[0:4, 0:64] = pat[...]
    for n in range(2):
        picked = jnp.sum(jnp.where((occurs > 0) & (ahead == n), number, 0.0), axis=0, keepdims=True)
        tab[4 + n : 5 + n, 0:32] = picked.astype(I32) - 1
    to_mids = pltpu.make_async_copy(tab, mids, m_copy)
    to_mids.start()

    to_mids.wait()

    def fill(s, _):
        k = mids[4 + lax.rem(s, 2), s // 2]
        block = modes[jnp.clip(k, 0, modes.shape[0] - 1)]
        send_m[s] = jnp.where(k >= 0, block, jnp.zeros_like(block))
        return 0

    lax.fori_loop(0, NQ, fill, 0, unroll=4)

    pl.semaphore_wait(barrier, 53)

    xf[own, pl.ds(2 * me, 2)] = send_m[pl.ds(2 * me, 2)]

    @pl.when(guest == 0)
    def _():
        away = remote(tab, patv, p_send, p_recv, (sib, y))
        away.start()
        here = pltpu.make_async_copy(tab, pats, p_copy)
        here.start()
        away.wait_send()
        here.wait()

    def other(cc):
        return lax.rem(cc + host, 2)

    def send_mode(dest, lands):
        remote(
            send_m.at[pl.ds(2 * dest, 2)], xf.at[lands, pl.ds(2 * me, 2)], sm_send, a_recv.at[p], (dest, y)
        ).start()

    def rows16(n):
        return pl.ds(pl.multiple_of(n * 16, 16), 16)

    def send_rec(q, cc):
        far = other(cc)
        remote(
            send_r.at[rows16(q * 2 + cc)], rbuf.at[rows16(32 * far + me)], r_send, r_recv,
            (q * 2 + host, y + far * (y3 - y)),
        ).start()

    send_mode(sib, 4 * (1 - guest))
    for dz, dx in FAR:
        q = chip_at(dz, dx)
        for cc in range(2):
            send_mode(q * 2 + cc, 4 * other(cc))

    lines = iota((128, 256), 0)
    facts = jnp.where(
        lines == 0, block_row[...], jnp.where(lines == 1, offset_row[...], jnp.where(lines == 2, owner_row[...], 0))
    ).astype(F32).astype(BF16)
    place = dot_nt(eye(256), facts)
    before = iota((256, 256), 0) < iota((256, 256), 1)
    same = place[:, 2:3] == owner_row[...].astype(F32)
    rank = jnp.sum(jnp.where(same & before, 1, 0), axis=0, keepdims=True)
    pos = owner_row[...] * SLOTS_E + rank
    place = place.astype(BF16)

    def permute(g, _):
        pick = jnp.where(iota((128, 256), 0) + g * 128 == pos, 1.0, 0.0).astype(BF16)
        at = pl.ds(pl.multiple_of(g * 128, 128), 128)
        send_r[at, 0:KW] = dot(pick, rec[...]).astype(BF16)
        send_r[at, KW:KA] = dot(pick, place).astype(BF16)
        return 0

    lax.fori_loop(0, 4, permute, 0)

    @pl.when(guest == 0)
    def _():
        rbuf[rows16(me)] = send_r[rows16(me)]

    remote(
        send_r.at[rows16(p * 2 + 1 - host)], rbuf.at[rows16(32 + me)], r_send, r_recv, (p * 2 + host, y3)
    ).start()

    @pl.when(guest == 1)
    def _():
        remote(send_r.at[rows16(sib)], rbuf.at[rows16(me)], r_send, r_recv, (sib, y)).start()

    def first(q, fresh):
        at = pl.ds(4 * q, 4)
        wait_bytes(fresh, a_recv.at[q])
        remote(
            xf.at[own, at], xf.at[1 + guest, at], b_send, b_recv.at[q],
            (me + guest * (sib - me), y1 + guest * (y3 - y1)),
        ).start()

        @pl.when(guest == 0)
        def _():
            remote(xf.at[0, at], xf.at[0, at], c_send, c_recv.at[0], (sib, y)).start()

    def second(q):
        at = pl.ds(4 * q, 4)
        wait_bytes(xf.at[1 + guest, at], b_recv.at[q])

        @pl.when(guest == 1)
        def _():
            remote(xf.at[2, at], xf.at[3, at], e_send, e_recv.at[q], (me, y1)).start()

        remote(xf.at[1 + guest, at], xf.at[1 + guest, at], c_send, c_recv.at[1 + guest], (sib, y)).start()

    def third(q):
        at = pl.ds(4 * q, 4)

        @pl.when(guest == 1)
        def _():
            wait_bytes(xf.at[3, at], e_recv.at[q])
            remote(xf.at[3, at], xf.at[3, at], c_send, c_recv.at[3], (sib, y)).start()

    chips = [p] + [chip_at((4 - dz) % 4, (4 - dx) % 4) for dz, dx in FAR]
    for n, q in enumerate(chips):
        first(q, xf.at[own, pl.ds(2 * sib, 2)] if n == 0 else xf.at[own, pl.ds(4 * q, 4)])
    for cc in (host, 1 - host):
        for dz, dx in FAR:
            send_rec(chip_at(dz, dx), cc)

    def place_matrix(n, _):
        ri = n // 6
        o = lax.rem(n, 6)
        k = lax.broadcasted_iota(I32, (256, 256), 0)
        col = lax.broadcasted_iota(I32, (256, 256), 1)
        bb = (col & 63) - 8 * o
        hit = (k == 32 * ri + (col >> 6) * 24 + bb) & (bb >= 0) & (bb < 24)
        ebuf[n] = jnp.where(hit, 1.0, 0.0).astype(BF16)
        return 0

    lax.fori_loop(0, 24, place_matrix, 0)

    for q in chips:
        second(q)
    for q in chips:
        third(q)

    @pl.when(guest == 1)
    def _():
        wait_bytes(patv, p_recv)
        here = pltpu.make_async_copy(patv, pats, p_copy)
        here.start()
        here.wait()

    @pl.when(guest == 0)
    def _():
        wait_bytes(rbuf.at[pl.ds(0, 31 * 16)], r_recv)

    @pl.when(guest == 1)
    def _():
        wait_bytes(rbuf.at[pl.ds(0, 32 * 16)], r_recv)

    mine = pl.ds(pl.multiple_of(512 * guest, 512), 512)
    remote(rbuf.at[mine], rbuf.at[mine], w_send, w_recv, (sib, y)).start()

    turned = eye(128)

    def transpose(k):
        def one(g, _):
            part = xf[k, pl.ds(32 * core + 4 * g, 4)].reshape(256, COLS)
            xt[k * 128 : k * 128 + 128, pl.ds(pl.multiple_of(g * 256, 256), 256)] = dot_nt(turned, part).astype(BF16)
            return 0

        lax.fori_loop(0, 8, one, 0, unroll=8)

    @pl.when(guest == 0)
    def _():
        wait_bytes(xf.at[2], c_recv.at[2])
        wait_bytes(xf.at[3], c_recv.at[3])

    @pl.when(guest == 1)
    def _():
        wait_bytes(xf.at[0], c_recv.at[0])
        wait_bytes(xf.at[1], c_recv.at[1])

    for k in range(4):
        transpose(k)

    pickrow = jnp.where(iota((8, 128), 0) == iota((8, 128), 1), 1.0, 0.0).astype(BF16)

    def collect(rows, last):
        facts = dot_nt(pickrow, rbuf[rows, KW:KA]).astype(I32)
        blk = facts[0:1]
        row = (blk >> 2) - 32 * core
        key = jnp.where((row >= 0) & (row < 32), facts[1:2] * 128 + (blk & 3) * 32 + row, -1)
        for o in range(6):
            pick = jnp.where(iota((128, 512), 0) + o * 128 == key, 1.0, 0.0).astype(BF16)
            part = dot(pick, rbuf[rows, :])
            if last:
                mbuf[o] = (half[o] + part).astype(BF16)
            else:
                half[o] = part

    collect(mine, False)
    wait_bytes(rbuf.at[pl.ds(pl.multiple_of(512 * (1 - guest), 512), 512)], w_recv)
    collect(pl.ds(pl.multiple_of(512 * (1 - guest), 512), 512), True)

    def assemble(v):
        for c in range(2):
            for w in range(2):
                acc = None
                for d in range(3):
                    if not 0 <= v - d <= 5:
                        continue
                    start = c * 576 + 96 * (w + 2 * d)
                    base = start // 128 * 128
                    ri = (start - base) // 32
                    term = dot(
                        mbuf[v - d, :, base : base + 256],
                        ebuf[ri * 6 + v - d],
                    )
                    acc = term if acc is None else acc + term
                acc = acc.astype(BF16)
                for a4 in range(4):
                    ks[c * 64 + 8 * v + 4 * w + a4] = jnp.concatenate(
                        [acc[j * 32 : j * 32 + 32, a4 * 64 : a4 * 64 + 64] for j in range(4)], axis=1
                    )

    for v in range(8):
        assemble(v)

    r0 = lax.broadcasted_iota(I32, (256, 256), 0)
    r1 = lax.broadcasted_iota(I32, (256, 256), 1)
    swap = jnp.where((r0 >> 4 == (r1 & 15)) & ((r0 & 15) == r1 >> 4), 1.0, 0.0).astype(BF16)

    def turn(n, _):
        arow = pl.ds(pl.multiple_of(n // 2 * 16, 16), 16)
        irow = pl.ds(pl.multiple_of(lax.rem(n, 2) * 16, 16), 16)
        part = ks[arow, irow, :].reshape(256, 256)
        lb[irow, arow, :] = dot(swap, part).astype(BF16).reshape(16, 16, 256)
        return 0

    lax.fori_loop(0, 16, turn, 0, unroll=8)

    def multiply(kinds):
        def one(i, _):
            ids = [pats[j, 32 * core + i] for j in range(4)]
            right_side = jnp.concatenate(
                [jnp.concatenate([xf[k, n] for n in ids], axis=0) for k in kinds], axis=1
            )
            out = dot(lb[i], right_side).astype(BF16)
            at = pl.ds(pl.multiple_of(i * 64, 64), 64)
            for n, k in enumerate(kinds):
                pb[k, at, 0:128] = out[0:64, n * 128 : n * 128 + 128]
                pb[k, at, 128:256] = out[64:128, n * 128 : n * 128 + 128]
            return 0

        lax.fori_loop(0, 32, one, 0, unroll=8)

    def gram(q):
        g = dot(xt[...], pb[q])
        for a in range(4):
            for b in range(8):
                at = pl.ds(pl.multiple_of(order[a] * 64 + (b // 2) * 16, 16), 16)
                gst[b % 2, q, at, :] = g[a * 128 + b * 16 : a * 128 + b * 16 + 16]
        remote(gst.at[1 - core, q], d0.at[q], d_send.at[q], d_recv.at[q], (sib, y)).start()

    def pair_sum(q):
        wait_bytes(d0.at[q], d_recv.at[q])
        hs[q - 1] = (gst[core, q] + d0[q]).astype(BF16)
        remote(hs.at[q - 1], hr.at[y], h_send.at[q - 1], h_recv.at[y], (me, order[q])).start()

    multiply((2, 3))
    gram(3)
    gram(2)
    pair_sum(3)
    multiply((0, 1))
    pair_sum(2)
    gram(1)
    pair_sum(1)
    gram(0)
    wait_bytes(d0.at[0], d_recv.at[0])
    total = gst[core, 0] + d0[0]
    for yy in (y2, y3, y1):
        wait_bytes(hr.at[yy], h_recv.at[yy])
        total = total + hr[yy].astype(F32)
    tot[...] = total.reshape(16, 16, 256)

    for dz, dx in FAR:
        q = chip_at(dz, dx)
        remote(tot.at[q], tr.at[p], t_send, t_recv, (q * 2 + core, y)).start()
    tr[p] = tot[p]
    wait_bytes(tr.at[pl.ds(0, 15)], t_recv)
    out[...] = jnp.sum(tr[...], axis=0)

    wait_bytes(send_m.at[pl.ds(0, 62)], sm_send)
    wait_bytes(rbuf.at[mine], w_send)
    wait_bytes(xf.at[0], b_send)
    wait_bytes(xf.at[pl.ds(0, 2)], c_send)

    @pl.when(guest == 0)
    def _():
        wait_bytes(send_r.at[pl.ds(0, 31 * 16)], r_send)

    @pl.when(guest == 1)
    def _():
        wait_bytes(send_r, r_send)
        wait_bytes(xf.at[0], e_send)

    for q in range(4):
        wait_bytes(d0.at[q], d_send.at[q])
    for q in range(3):
        wait_bytes(hs.at[q], h_send.at[q])
    wait_bytes(tot.at[pl.ds(0, 15)], t_send)


def body(elem_records, elem_owner, elem_block, elem_offset, modes, mode_readers, pattern):
    dma = pltpu.SemaphoreType.DMA
    vm = pl.BlockSpec(memory_space=pltpu.VMEM)
    out = pl.pallas_call(
        kernel,
        out_shape=jax.ShapeDtypeStruct((16, 256), F32),
        in_specs=[vm] * 7,
        out_specs=vm,
        scratch_shapes=[
            pltpu.VMEM((NQ, BS, COLS), BF16),
            pltpu.VMEM((5, NQ, BS, COLS), BF16),
            pltpu.VMEM((512, KA), BF16),
            pltpu.VMEM((1024, KA), BF16),
            pltpu.VMEM((24, 256, 256), BF16),
            pltpu.VMEM((6, 128, KA), BF16),
            pltpu.VMEM((128, 32, 256), BF16),
            pltpu.VMEM((32, 128, 256), BF16),
            pltpu.VMEM((512, 2048), BF16),
            pltpu.VMEM((4, 2048, 256), BF16),
            pltpu.VMEM((2, 4, 256, 256), F32),
            pltpu.VMEM((4, 256, 256), F32),
            pltpu.VMEM((3, 256, 256), BF16),
            pltpu.VMEM((4, 256, 256), BF16),
            pltpu.VMEM((16, 16, 256), F32),
            pltpu.VMEM((16, 16, 256), F32),
            dma, dma((16,)), dma, dma, dma, dma, dma, dma((16,)), dma, dma((4,)),
            dma, dma((16,)), dma((4,)), dma((4,)), dma((3,)), dma((4,)), dma, dma,
            pltpu.VMEM((8, 128), I32), pltpu.VMEM((8, 128), I32), pltpu.SMEM((8, 128), I32), pltpu.SMEM((8, 128), I32),
            dma, dma, dma, dma, pltpu.VMEM((6, 128, KA), F32),
        ],
        compiler_params=pltpu.CompilerParams(
            collective_id=0, has_side_effects=True, vmem_limit_bytes=60 << 20
        ),
        name="sweep",
    )(
        pattern.T, elem_records, elem_owner.T, elem_block.reshape(1, 256), elem_offset.reshape(1, 256),
        modes, mode_readers.T,
    )
    return out[:, 0:128], out[:, 128:256]


def solution(mesh):
    in_specs = (
        P(("sub", "col"), None),
        P(("sub", "col"), None),
        P(("sub", "col")),
        P(("sub", "col")),
        P("sub", None, "col"),
        P("sub", None),
        P("sub", None),
    )
    out_specs = (P("sub", "col"), P("sub", "col"))
    return jax.shard_map(body, mesh=mesh, in_specs=in_specs, out_specs=out_specs, check_vma=False)
```
